32 devices in a mesh: groups: 2 (over x), ctx: 16 (over z, y, core).
Axes of the slice: x: 2, y: 2, z: 4, core: 2. Of those that a mesh axis runs over, the one named last changes fastest.
Arguments:
- index_queries: bfloat16 [64, 32, 128], P(('groups', 'ctx')), parts along dimension 0, may hold values from -0.5 to 0.5
- index_weights: bfloat16 [64, 32], P(('groups', 'ctx')), parts along dimension 0, may hold values from -1 to 1
- index_keys: bfloat16 [16384, 128], P(('groups', 'ctx')), parts along dimension 0, may hold values from -4 to 4
- key_scales: bfloat16 [16384], P(('groups', 'ctx')), parts along dimension 0, may hold values from 0.25 to 4
- q_latent: bfloat16 [64, 128, 576], P(('groups', 'ctx')), parts along dimension 0, may hold values from -6 to 6
- latents: bfloat16 [16384, 576], P(('groups', 'ctx')), parts along dimension 0, may hold values from -4 to 4
- wanted: int32 [32, 16, 4], P(('groups', 'ctx')), parts along dimension 0, may hold values from -1 to 7, as said below
- selected: int32 [64, 2048], P(('groups', 'ctx')), parts along dimension 0, may hold values from 0 to 4095, as said below
Outputs:
- index_scores: float32 [64, 8192], P(('groups', 'ctx')), parts along dimension 0
- attended: bfloat16 [64, 128, 512], P(('groups', 'ctx')), parts along dimension 0
The draws below stay inside these ranges and needn't reach their ends.
There are 2 independent parts, one for each index of `groups`. The reference program is written for one: setup_inputs(seed, part) draws one part's arguments, and reference() takes and returns one part's arrays. A program takes and returns all parts, laid end to end along the dimension named above; each array names one. Nothing has to cross between parts.
Inputs may be any that keep to these rules, and one draw needn't show every extreme that they name: For each device r and owner o, the first n entries of wanted[r, o, :] are distinct block numbers of that owner, with n from 1 to 4, and the remaining entries are -1; in every draw some owner is asked for 4 blocks by every device. `selected`: the 2048 entries of a row are distinct, and each names a slot row whose block entry in wanted is not -1.
All inputs are finite; a program needn't handle non-finite values.
Results may differ from the reference program's by a relative error of at most 0.0046.
Values may be sent and summed in bfloat16 or wider, within the bound.
No kernel may reach another device: no remote copies, remote signals or barrier semaphores. Data moves between devices by JAX's collectives and lax.ppermute only.
A program may use at most 128 MiB of HBM per device.

```python
import math
import jax
import jax.numpy as jnp
from jax import lax

H = 128
KVR = 512
ROPE = 64
IH = 32
IDX_DIM = 128
TOPK = 2048
BLOCK = 64
MAXB = 4
Q_DEV = 2
CTX_DEV = 512
QUERIES = 32
CONTEXT = 8192
N_CTX = 16


def request_plan(key):
    key_hot, key_cold, key_order, key_pick = jax.random.split(jax.random.fold_in(key, 11), 4)
    hot_count = N_CTX // 4
    owner_blocks = CTX_DEV // BLOCK
    needed = -(-(2 * (TOPK // BLOCK) - hot_count * MAXB) // (N_CTX - hot_count))
    cold_floor = min(MAXB - 1, max(1, needed))
    shuffled = jax.random.permutation(key_hot, N_CTX)
    owner_rank = jnp.argsort(shuffled)
    is_hot = owner_rank < hot_count
    extra = (jax.random.randint(key_cold, (N_CTX, N_CTX), 0, 4) == 0).astype(jnp.int32)
    counts = jnp.where(is_hot[None, :], MAXB, jnp.minimum(cold_floor + extra, MAXB)).astype(jnp.int32)
    order_keys = jax.random.randint(key_order, (N_CTX, N_CTX, owner_blocks), 0, 1 << 16) * owner_blocks + jnp.arange(owner_blocks, dtype=jnp.int32)
    ordering = jnp.argsort(order_keys, axis=-1)[..., :MAXB].astype(jnp.int32)
    slot_index = jnp.arange(MAXB, dtype=jnp.int32)
    wanted = jnp.where(slot_index[None, None, :] < counts[..., None], ordering, -1).astype(jnp.int32)
    slot_count = N_CTX * MAXB * BLOCK
    slot_ids = jnp.arange(slot_count, dtype=jnp.int32)
    slot_owner = slot_ids // (MAXB * BLOCK)
    slot_number = slot_ids // BLOCK % MAXB
    live = (slot_number[None, :] < counts[:, slot_owner]).astype(jnp.int32)
    requester = jnp.arange(Q_DEV * N_CTX, dtype=jnp.int32) // Q_DEV
    live_rows = live[requester]
    noise = jax.random.randint(key_pick, (Q_DEV * N_CTX, slot_count), 0, 1024)
    priority = live_rows * (1024 * slot_count) + noise * slot_count + slot_ids[None, :]
    selected = lax.top_k(priority, TOPK)[1].astype(jnp.int32)
    return (wanted, selected)


def draw_wanted(key, part):
    plan = request_plan(key)
    return plan[0]


def draw_selected(key, part):
    plan = request_plan(key)
    return plan[1]


def draw_latents(key, part):
    key = jax.random.fold_in(key, 21)
    values = jnp.clip(jax.random.normal(key, (CONTEXT, KVR + ROPE)), -4.0, 4.0)
    return values.astype(jnp.bfloat16)


def draw_q_latent(key, part):
    key = jax.random.fold_in(key, 22)
    values = jnp.clip(1.3 * jax.random.normal(key, (Q_DEV * N_CTX, H, KVR + ROPE)), -6.0, 6.0)
    return values.astype(jnp.bfloat16)


def level_of(stream_key, dims, shards, least, largest):
    factor_of, own = 1.0, jax.random.fold_in(stream_key, 6)
    for dim, parts in shards:
        steps = jnp.exp(jax.random.uniform(jax.random.fold_in(own, dim), (parts,), jnp.float32, least / len(shards), largest / len(shards)))
        factor_of = factor_of * jnp.repeat(steps, dims[dim] // parts).reshape([-1 if axis == dim else 1 for axis in range(len(dims))])
    return factor_of


def bell_draw(own_key, extent, spread, reach, cuts=(), held_as=jnp.bfloat16):
    result = spread * jax.random.normal(own_key, extent, jnp.float32)
    if cuts:
        result = result * level_of(own_key, extent, cuts, -0.22, 0.18)
    return jnp.clip(result, -reach, reach).astype(held_as)


def setup_inputs(seed: int = 0, part: int = 0) -> dict:
    streams_of = jax.random.split(jax.random.key(seed), 9)
    part_splits = jax.random.split(jax.random.fold_in(streams_of[8], part), 9)
    return {
        "index_queries": bell_draw(part_splits[0], (QUERIES, IH, IDX_DIM), IDX_DIM ** -0.5, 0.5, ((0, 16),)),
        "index_weights": bell_draw(part_splits[1], (QUERIES, IH), IH ** -0.5, 1.0, ((0, 16),)),
        "index_keys": bell_draw(part_splits[2], (CONTEXT, IDX_DIM), 1.0, 4.0, ((0, 16),)),
        "key_scales": jnp.clip(jnp.exp(math.log(4.0) - 2.7725887 * jax.random.uniform(part_splits[3], (CONTEXT,), jnp.float32) ** level_of(part_splits[3], (CONTEXT,), ((0, 16),), -0.2, 0.2)), 0.25, 4.0).astype(jnp.bfloat16),
        "q_latent": draw_q_latent(jax.random.fold_in(jax.random.fold_in(streams_of[8], part), 71), part),
        "latents": draw_latents(jax.random.fold_in(jax.random.fold_in(streams_of[8], part), 71), part),
        "wanted": draw_wanted(jax.random.fold_in(jax.random.fold_in(streams_of[8], part), 71), part),
        "selected": draw_selected(jax.random.fold_in(jax.random.fold_in(streams_of[8], part), 71), part),
    }


softmax_scale = 192.0 ** -0.5


def reference(index_queries, index_weights, index_keys, key_scales, q_latent, latents, wanted, selected):
    queries_full = index_queries.astype(jnp.float32)
    weights_full = index_weights.astype(jnp.float32)
    block_size = math.gcd(CONTEXT, 1024)
    key_blocks = index_keys.reshape(CONTEXT // block_size, block_size, IDX_DIM)
    scale_blocks = key_scales.reshape(CONTEXT // block_size, block_size)

    def index_block(operands):
        key_rows, scale_rows = operands
        raw = jnp.einsum("tjd,sd->tjs", queries_full, key_rows.astype(jnp.float32), precision=lax.Precision.HIGHEST)
        lifted = jax.nn.relu(raw * scale_rows.astype(jnp.float32)[None, None, :])
        return jnp.einsum("tj,tjs->ts", weights_full, lifted, precision=lax.Precision.HIGHEST)

    blocks = lax.map(index_block, (key_blocks, scale_blocks))
    index_scores = jnp.moveaxis(blocks, 0, 1).reshape(QUERIES, CONTEXT)

    owner = selected // (MAXB * BLOCK)
    slot_number = (selected // BLOCK) % MAXB
    inner = selected % BLOCK
    requester = (jnp.arange(QUERIES, dtype=jnp.int32) // Q_DEV)[:, None]
    block_number = wanted[requester, owner, slot_number]
    token_rows = (owner * CTX_DEV + block_number * BLOCK + inner).astype(jnp.int32)

    def attend(operands):
        query_row, chosen = operands
        picked_rows = jnp.take(latents, chosen, axis=0)
        logits = jnp.dot(query_row, picked_rows.T, preferred_element_type=jnp.float32) * softmax_scale
        highest = jnp.max(logits, axis=1, keepdims=True)
        expo = jnp.exp(logits - highest)
        weights_low = (expo / jnp.sum(expo, axis=1, keepdims=True)).astype(jnp.bfloat16)
        return jnp.dot(weights_low, picked_rows[:, :KVR], preferred_element_type=jnp.float32).astype(jnp.bfloat16)

    attended = lax.map(attend, (q_latent, token_rows))
    return (index_scores, attended)
```

```python
import functools

import jax
import jax.numpy as jnp
from jax import lax
from jax.experimental import pallas as pl
from jax.experimental.pallas import tpu as pltpu
from jax.sharding import PartitionSpec as P

BLOCK = 64
LANES = 512
KVR = 512
ROPE = 64
HEADS = 128
IH = 32
IDX = 128
TOK = 512
NEG = -1e30
LOG2E = 1.4426950408889634
TO_LOG2 = 192.0 ** (-0.5) * LOG2E

KV_ROPE = TOK
KV_KEYS = KV_ROPE + ROPE
KV_SCALE = KV_KEYS + IDX
KV_ROWS = KV_SCALE + 16

Q_LAT = 2 * HEADS
Q_ROPE = Q_LAT
Q_IDX = Q_ROPE + 32
Q_W = Q_IDX + 16
Q_BIAS = Q_W + 16

BF = jnp.bfloat16
F32 = jnp.float32
VMEM = pl.BlockSpec(memory_space=pltpu.VMEM)


def nn(a, b):
    return lax.dot_general(a, b, (((1,), (0,)), ((), ())), preferred_element_type=F32)


def nt(a, b):
    return lax.dot_general(a, b, (((1,), (1,)), ((), ())), preferred_element_type=F32)


def iota(shape, dim):
    return lax.broadcasted_iota(jnp.int32, shape, dim)


def onehot(cond):
    return jnp.where(cond, 1.0, 0.0).astype(BF)


def eye(n):
    return onehot(iota((n, n), 0) == iota((n, n), 1))


def pack_kv_kernel(lat_ref, keys_ref, scale_ref, out_ref):
    out_ref[0:TOK, :] = lat_ref[:, 0:KVR]
    out_ref[KV_ROPE:KV_KEYS, :] = nt(eye(ROPE), lat_ref[:, KVR : KVR + ROPE]).astype(BF)
    out_ref[KV_KEYS:KV_SCALE, :] = nt(eye(IDX), keys_ref[...]).astype(BF)
    out_ref[KV_SCALE:KV_ROWS, :] = jnp.broadcast_to(scale_ref[...], (16, TOK))


def pack_q_kernel(half_size, q_ref, iq_ref, w_ref, sel_ref, want_ref, wire_ref, own_ref, bias):
    me = lax.axis_index("ctx")
    half = me // half_size
    n = 2 * half_size
    slots = want_ref.shape[2]
    topk = sel_ref.shape[1]
    for t in range(2):
        wire_ref[t * HEADS : (t + 1) * HEADS, :] = q_ref[t, :, 0:KVR]
    place = [
        onehot(iota((ROPE, 2 * ROPE), 0) + t * ROPE == iota((ROPE, 2 * ROPE), 1)) for t in range(2)
    ]
    ropes = nn(q_ref[0, :, KVR : KVR + ROPE], place[0]) + nn(q_ref[1, :, KVR : KVR + ROPE], place[1])
    ropes = ropes.astype(BF)
    for b in range(4):
        wire_ref[Q_ROPE : Q_ROPE + 32, b * 128 : (b + 1) * 128] = ropes[b * 32 : (b + 1) * 32, :]
        wire_ref[Q_IDX : Q_IDX + 16, b * 128 : (b + 1) * 128] = iq_ref[
            b // 2, (b % 2) * 16 : (b % 2) * 16 + 16, :
        ]
    wire_ref[Q_W : Q_W + 16, :] = jnp.zeros((16, LANES), BF)
    wire_ref[Q_W : Q_W + 2, 0:IH] = w_ref[...]
    lane_block = iota((n, LANES), 1) // BLOCK
    spread = onehot(iota((BLOCK, LANES), 1) % BLOCK == iota((BLOCK, LANES), 0))
    for t in range(2):
        sel = sel_ref[t : t + 1, :]
        slot = sel // BLOCK
        inner = onehot(sel % BLOCK == iota((BLOCK, topk), 0))
        total = jnp.zeros((n, LANES), F32)
        for b in range(slots):
            picked = onehot(slot == iota((n, topk), 0) * slots + b)
            count = nt(picked, inner)
            wide = nn(count.astype(BF), spread)
            total = total + jnp.where(lane_block == want_ref[0, :, b : b + 1], wide, 0.0)
        bias[t] = jnp.where(total > 0.5, 0.0, NEG)
    mine = half * half_size
    other = (1 - half) * half_size
    for t in range(2):
        own_ref[t * half_size : (t + 1) * half_size, :] = bias[
            t, pl.ds(pl.multiple_of(mine, half_size), half_size), :
        ].astype(BF)
        wire_ref[Q_BIAS + t * half_size : Q_BIAS + (t + 1) * half_size, :] = bias[
            t, pl.ds(pl.multiple_of(other, half_size), half_size), :
        ].astype(BF)


def split3(x):
    hi = x.astype(BF)
    rest = x - hi.astype(F32)
    mid = rest.astype(BF)
    return hi, mid, (rest - mid.astype(F32)).astype(BF)


def attend_kernel(half_size, masks, first, mode, *refs):
    count = len(masks)
    refs = list(refs)
    q_ref, bias_ref = refs[:2]
    pieces = refs[2 : 2 + count]
    pos = 2 + count
    if not first:
        acc_in, m_in, l_in, sc_in = refs[pos : pos + 4]
        pos += 4
    if mode == "state":
        acc_out, m_out, l_out, sc_out = refs[pos : pos + 4]
        pos += 4
    elif mode == "wire":
        wire_out = refs[pos]
        pos += 1
    else:
        o_out, lse_out, sc_out = refs[pos : pos + 3]
        pos += 3
    bias, logits, sc = refs[pos : pos + 3]

    me = lax.axis_index("ctx")
    core = me % 2
    rows = 2 * half_size
    bias_base = Q_BIAS if bias_ref.shape[0] > rows else 0
    bias[...] = bias_ref[bias_base : bias_base + rows, :].astype(F32)
    if not first:
        sc[...] = sc_in[...]
    elif len(masks) < half_size:
        sc[...] = jnp.zeros_like(sc)

    q_lat = q_ref[0:Q_LAT, :]
    ropes = jnp.concatenate(
        [q_ref[Q_ROPE : Q_ROPE + 32, b * 128 : (b + 1) * 128] for b in range(4)], axis=0
    )
    place = [
        onehot(iota((ROPE, 2 * ROPE), 0) + t * ROPE == iota((ROPE, 2 * ROPE), 1)) for t in range(2)
    ]
    q_rope = jnp.concatenate([nt(ropes, place[t]) for t in range(2)], axis=0).astype(BF)
    iq = jnp.concatenate(
        [q_ref[Q_IDX : Q_IDX + 16, b * 128 : (b + 1) * 128] for b in range(4)], axis=0
    )
    w_cols = nt(eye(IH), q_ref[Q_W : Q_W + 16, 0:IH])

    m_prev = None if first else m_in[:, 0:1]
    m_new = m_prev
    for p in range(count):
        kv = pieces[p]
        src = lax.bitwise_xor(me, jnp.where(core == 0, masks[p][0], masks[p][1]))
        src = src % half_size
        s = nt(q_lat, kv[0:TOK, :]) + nn(q_rope, kv[KV_ROPE:KV_KEYS, :])
        s = s * TO_LOG2
        for t in range(2):
            part = s[t * HEADS : (t + 1) * HEADS, :] + bias[pl.ds(t * half_size + src, 1), :]
            logits[t * HEADS : (t + 1) * HEADS, p * TOK : (p + 1) * TOK] = part
        raw = nn(iq, kv[KV_KEYS:KV_SCALE, :])
        scale = kv[KV_SCALE : KV_SCALE + 16, :].astype(F32)[0:1, :]
        lifted = jnp.maximum(raw, 0.0)
        for t in range(2):
            weighted = lifted[t * IH : (t + 1) * IH, :] * w_cols[:, t : t + 1]
            sc[pl.ds(t * half_size + src, 1), :] = jnp.sum(weighted, axis=0, keepdims=True) * scale
    top = jnp.max(logits[...], axis=1, keepdims=True)
    m_new = top if first else jnp.maximum(m_prev, top)

    total = None
    acc = None
    for p in range(count):
        e = jnp.exp2(logits[:, p * TOK : (p + 1) * TOK] - m_new)
        part = jnp.sum(e, axis=1, keepdims=True)
        total = part if total is None else total + part
        out = nn(e.astype(BF), pieces[p][0:TOK, :])
        acc = out if acc is None else acc + out
    if not first:
        alpha = jnp.exp2(m_prev - m_new)
        total = total + l_in[:, 0:1] * alpha
        acc = acc + acc_in[...] * alpha
    if mode == "state":
        acc_out[...] = acc
        m_out[...] = jnp.broadcast_to(m_new, m_out.shape)
        l_out[...] = jnp.broadcast_to(total, l_out.shape)
        sc_out[...] = sc[...]
        return
    norm = acc / total
    lse = m_new + jnp.log(total) * LOG2E
    if mode == "own":
        o_out[...] = norm
        lse_out[...] = jnp.broadcast_to(lse, lse_out.shape)
        sc_out[...] = sc[...]
        return
    wire_out[0:Q_LAT, :] = norm.astype(BF)
    diag = iota((Q_LAT, Q_LAT), 0) == iota((Q_LAT, Q_LAT), 1)
    row = jnp.sum(jnp.where(diag, lse, 0.0), axis=0, keepdims=True)
    hi, mid, lo = [x.astype(F32) for x in split3(row)]
    which = iota((16, Q_LAT), 0)
    left = jnp.where(which == 0, hi, jnp.where(which == 1, lo, 0.0))
    right = jnp.where(which == 0, mid, 0.0)
    wire_out[Q_LAT : Q_LAT + 16, 0:Q_LAT] = left.astype(BF)
    wire_out[Q_LAT : Q_LAT + 16, Q_LAT : 2 * Q_LAT] = right.astype(BF)
    hi, mid, lo = split3(sc[...])
    wire_out[Q_LAT + 16 : Q_LAT + 16 + rows, :] = hi
    wire_out[Q_LAT + 16 + rows : Q_LAT + 16 + 2 * rows, :] = mid


def final_kernel(half_size, o_ref, lse_ref, sc_ref, wire_ref, scores_ref, out_ref):
    me = lax.axis_index("ctx")
    half = me // half_size
    rows = 2 * half_size
    stats = wire_ref[Q_LAT : Q_LAT + 16, :].astype(F32)
    row = stats[0:1, 0:Q_LAT] + stats[0:1, Q_LAT : 2 * Q_LAT] + stats[1:2, 0:Q_LAT]
    diag = iota((Q_LAT, Q_LAT), 0) == iota((Q_LAT, Q_LAT), 1)
    lse_r = jnp.sum(jnp.where(diag, row, 0.0), axis=1, keepdims=True)
    lse_o = lse_ref[:, 0:1]
    top = jnp.maximum(lse_r, lse_o)
    e_r = jnp.exp2(lse_r - top)
    e_o = jnp.exp2(lse_o - top)
    inv = 1.0 / (e_r + e_o)
    out = o_ref[...] * (e_o * inv) + wire_ref[0:Q_LAT, :].astype(F32) * (e_r * inv)
    for t in range(2):
        out_ref[t] = out[t * HEADS : (t + 1) * HEADS, :].astype(BF)
    base = Q_LAT + 16
    sc_r = wire_ref[base : base + rows, :].astype(F32) + wire_ref[
        base + rows : base + 2 * rows, :
    ].astype(F32)
    sc_o = sc_ref[...]
    for t in range(2):
        for d in range(half_size):
            line = t * half_size + d
            at = pl.multiple_of((half * half_size + d) * TOK, TOK)
            scores_ref[t : t + 1, pl.ds(at, TOK)] = sc_o[line : line + 1, :]
            at = pl.multiple_of(((1 - half) * half_size + d) * TOK, TOK)
            scores_ref[t : t + 1, pl.ds(at, TOK)] = sc_r[line : line + 1, :]


def call(kernel, out_shape, name, flops, *args, scratch=(), aliases=None):
    moved = sum(a.size * a.dtype.itemsize for a in args)
    return pl.pallas_call(
        kernel,
        out_shape=out_shape,
        in_specs=[VMEM] * len(args),
        out_specs=jax.tree.map(lambda _: VMEM, out_shape),
        scratch_shapes=list(scratch),
        input_output_aliases=aliases or {},
        name=name,
        cost_estimate=pl.CostEstimate(flops=int(flops), bytes_accessed=moved, transcendentals=0),
        compiler_params=pltpu.CompilerParams(vmem_limit_bytes=48 << 20),
    )(*args)


def shape(dims, dtype):
    return jax.ShapeDtypeStruct(dims, dtype)


def attend(half_size, q_wire, bias, group, state, mode, name):
    masks = tuple(mask for _, mask in group)
    args = [q_wire, bias] + [piece for piece, _ in group]
    aliases = {}
    rows = 2 * half_size
    state_shape = (
        shape((Q_LAT, KVR), F32),
        shape((Q_LAT, 128), F32),
        shape((Q_LAT, 128), F32),
        shape((rows, LANES), F32),
    )
    if state is not None:
        args += list(state)
    if mode == "state":
        outs = state_shape
    elif mode == "wire":
        outs = shape((Q_LAT + 16 + 2 * rows, LANES), BF)
    else:
        outs = (state_shape[0], state_shape[1], state_shape[3])
    scratch = [
        pltpu.VMEM((rows, LANES), F32),
        pltpu.VMEM((Q_LAT, TOK * len(group)), F32),
        pltpu.VMEM((rows, LANES), F32),
    ]
    flops = 2 * Q_LAT * TOK * len(group) * (2 * KVR + ROPE)
    return call(
        functools.partial(attend_kernel, half_size, masks, state is None, mode),
        outs,
        name,
        flops,
        *args,
        scratch=scratch,
        aliases=aliases,
    )


def local(n, index_queries, index_weights, index_keys, key_scales, q_latent, latents, wanted, selected):
    half_size = n // 2
    bits = n.bit_length() - 1
    top = 1 << (bits - 1)

    def permute(x, move):
        return lax.ppermute(x, "ctx", [(i, move(i)) for i in range(n)])

    def swap(x):
        return permute(x, lambda i: i ^ 1)

    kv = call(
        pack_kv_kernel,
        shape((KV_ROWS, LANES), BF),
        "pack_kv",
        2 * TOK * TOK * 192,
        latents,
        index_keys,
        key_scales.reshape(1, TOK),
    )
    r1 = permute(kv, lambda i: i ^ 2 if i % 2 == 0 else i ^ 4)
    r2 = permute(kv, lambda i: i ^ 4 if i % 2 == 0 else i ^ 2)
    r3 = permute(r1, lambda i: i ^ 4 if i % 2 == 0 else i ^ 2)
    held = [(kv, (0, 0)), (r1, (2, 4)), (r2, (4, 2)), (r3, (6, 6))]
    for bit in range(3, bits - 1):
        step = 1 << bit
        held = held + [
            (permute(piece, lambda i: i ^ step), (a ^ step, b ^ step)) for piece, (a, b) in held
        ]

    rows = 2 * half_size
    q_wire, bias_own = call(
        functools.partial(pack_q_kernel, half_size),
        (shape((Q_BIAS + rows, LANES), BF), shape((rows, LANES), BF)),
        "pack_q",
        2 * 2 * n * 2048 * 64 * 4,
        q_latent,
        index_queries,
        index_weights,
        selected,
        wanted,
        scratch=[pltpu.VMEM((2, n, LANES), F32)],
    )
    q_far = permute(q_wire, lambda i: i ^ top)

    pairs = []
    for piece, (a, b) in held:
        pairs.append([(piece, (a, b)), (swap(piece), (1 ^ b, 1 ^ a))])
    groups = [pairs[0] + pairs[1] + pairs[2], pairs[3]]
    for at in range(4, len(pairs), 3):
        groups.append(sum(pairs[at : at + 3], []))

    def run(q, bias, last, name):
        state = None
        for k, group in enumerate(groups):
            mode = last if k == len(groups) - 1 else "state"
            state = attend(half_size, q, bias, group, state, mode, f"{name}_{k}")
        return state

    wire = run(q_far, q_far, "wire", "attend_far")
    o_far = permute(wire, lambda i: i ^ top)
    o_own, lse_own, scores_own = run(q_wire, bias_own, "own", "attend_own")
    scores, attended = call(
        functools.partial(final_kernel, half_size),
        (shape((2, n * TOK), F32), shape((2, HEADS, KVR), BF)),
        "combine",
        Q_LAT * KVR * 4,
        o_own,
        lse_own,
        scores_own,
        o_far,
    )
    return scores, attended


def solution(mesh):
    spec = P(("groups", "ctx"))
    return jax.shard_map(
        functools.partial(local, mesh.shape["ctx"]),
        mesh=mesh,
        in_specs=(spec,) * 8,
        out_specs=(spec, spec),
        check_vma=False,
    )
```

```python
import functools

import jax
import jax.numpy as jnp
from jax import lax
from jax.experimental import pallas as pl
from jax.experimental.pallas import tpu as pltpu
from jax.sharding import PartitionSpec as P

BLOCK = 64
LANES = 512
KVR = 512
ROPE = 64
HEADS = 128
IH = 32
IDX = 128
TOK = 512
NEG = -1e30
LOG2E = 1.4426950408889634
TO_LOG2 = 192.0 ** (-0.5) * LOG2E

WIDTH = KVR + ROPE
ROWS = 2 * HEADS
CHUNKS = TOK // 128

I_W = 2 * IH
I_ROWS = I_W + 16
K_ROWS = TOK + 16

Q_IDX = 2 * WIDTH
Q_BIAS = Q_IDX + I_ROWS

BF = jnp.bfloat16
F32 = jnp.float32
VMEM = pl.BlockSpec(memory_space=pltpu.VMEM)
HBM = pl.BlockSpec(memory_space=pltpu.HBM)


def nn(a, b):
    return lax.dot_general(a, b, (((1,), (0,)), ((), ())), preferred_element_type=F32)


def nt(a, b):
    return lax.dot_general(a, b, (((1,), (1,)), ((), ())), preferred_element_type=F32)


def iota(shape, dim):
    return lax.broadcasted_iota(jnp.int32, shape, dim)


def onehot(cond):
    return jnp.where(cond, 1.0, 0.0).astype(BF)


def eye(n):
    return onehot(iota((n, n), 0) == iota((n, n), 1))


def pack_kernel(
    half_size, q_in, iq_in, w_in, keys_in, scale_in, sel_in, want_in, lat_in,
    wire_ref, own_ref, k_ref, lat_ref, w_ref, scale_ref, sel_ref, want_ref, bias, sems,
):
    moves = [
        (sel_in, sel_ref),
        (want_in, want_ref),
        (w_in, w_ref),
        (scale_in, scale_ref),
        (q_in, wire_ref.at[0:Q_IDX]),
        (iq_in, wire_ref.at[Q_IDX : Q_IDX + I_W]),
        (keys_in, k_ref.at[0:TOK]),
        (lat_in, lat_ref),
    ]
    copies = [
        pltpu.make_async_copy(src, dst, sems.at[k]) for k, (src, dst) in enumerate(moves)
    ]
    for copy in copies:
        copy.start()
    wire_ref[Q_IDX + I_W : Q_BIAS, :] = jnp.zeros((16, IDX), BF)
    k_ref[TOK:K_ROWS, :] = jnp.zeros((16, IDX), BF)
    for copy in copies[:4]:
        copy.wait()
    wire_ref[Q_IDX + I_W : Q_IDX + I_W + 2, 0:IH] = w_ref[...]
    k_ref[TOK : TOK + CHUNKS, :] = scale_ref[...]
    me = lax.axis_index("ctx")
    half = me // half_size
    n = 2 * half_size
    slots = want_ref.shape[0]
    topk = sel_ref.shape[1]
    asked = nt(eye(n), want_ref[...].astype(F32).astype(BF))
    lane_block = (iota((n, LANES), 1) // BLOCK).astype(F32)
    spread = onehot(iota((BLOCK, LANES), 1) % BLOCK == iota((BLOCK, LANES), 0))
    line = iota((slots * n, topk), 0)
    slot_of_line = (line % n) * slots + line // n
    for t in range(2):
        sel = sel_ref[t : t + 1, :]
        inner = onehot(sel % BLOCK == iota((BLOCK, topk), 0))
        count = nt(onehot(sel // BLOCK == slot_of_line), inner)
        wide = nn(count.astype(BF), spread)
        total = jnp.zeros((n, LANES), F32)
        for b in range(slots):
            total = total + jnp.where(
                lane_block == asked[:, b : b + 1], wide[b * n : (b + 1) * n, :], 0.0
            )
        bias[t] = jnp.where(total > 0.5, 0.0, NEG)
    mine = pl.multiple_of(half * half_size, half_size)
    other = pl.multiple_of((1 - half) * half_size, half_size)
    rows = 2 * half_size
    for c in range(CHUNKS):
        lanes = slice(c * 128, (c + 1) * 128)
        own_ref[c * rows : (c + 1) * rows, :] = jnp.concatenate(
            [bias[t, pl.ds(mine, half_size), lanes] for t in range(2)], axis=0
        ).astype(BF)
        wire_ref[Q_BIAS + c * rows : Q_BIAS + (c + 1) * rows, :] = jnp.concatenate(
            [bias[t, pl.ds(other, half_size), lanes] for t in range(2)], axis=0
        ).astype(BF)
    for copy in copies[4:]:
        copy.wait()


def unpack_kernel(half_size, own_ref, wire_ref, bias_ref, q_ref, out_ref, *more):
    for t in range(2):
        rows = nt(eye(HEADS), wire_ref[t * WIDTH : (t + 1) * WIDTH, :])
        q_ref[t * HEADS : (t + 1) * HEADS, :] = rows.astype(BF)
    rows = 2 * half_size
    base = bias_ref.shape[0] - CHUNKS * rows
    for c in range(CHUNKS):
        out_ref[:, c * 128 : (c + 1) * 128] = bias_ref[
            base + c * rows : base + (c + 1) * rows, :
        ].astype(F32)
    if more:
        (pair_ref,) = more
        pair_ref[0:I_ROWS, :] = own_ref[Q_IDX:Q_BIAS, :]
        pair_ref[I_ROWS : 2 * I_ROWS, :] = wire_ref[Q_IDX:Q_BIAS, :]


def split3(x):
    hi = x.astype(BF)
    rest = x - hi.astype(F32)
    mid = rest.astype(BF)
    return hi, mid, (rest - mid.astype(F32)).astype(BF)


def attend_kernel(half_size, masks, first, mode, *refs):
    count = len(masks)
    refs = list(refs)
    q_ref, bias_ref = refs[:2]
    pieces = refs[2 : 2 + count]
    pos = 2 + count
    if not first:
        acc_in, m_in, l_in = refs[pos : pos + 3]
        pos += 3
    outs = refs[pos:-1]
    logits = refs[-1]

    me = lax.axis_index("ctx")
    core = me % 2
    q = q_ref[...]
    m_prev = None if first else m_in[:, 0:1]
    m_new = m_prev
    for p in range(count):
        kv = pieces[p]
        src = lax.bitwise_xor(me, jnp.where(core == 0, masks[p][0], masks[p][1]))
        src = src % half_size
        s = nn(q, kv[0:WIDTH, :]) * TO_LOG2
        for t in range(2):
            part = s[t * HEADS : (t + 1) * HEADS, :] + bias_ref[pl.ds(t * half_size + src, 1), :]
            logits[t * HEADS : (t + 1) * HEADS, p * TOK : (p + 1) * TOK] = part
    top = jnp.max(logits[...], axis=1, keepdims=True)
    m_new = top if first else jnp.maximum(m_prev, top)

    total = None
    acc = None
    for p in range(count):
        e = jnp.exp2(logits[:, p * TOK : (p + 1) * TOK] - m_new)
        part = jnp.sum(e, axis=1, keepdims=True)
        total = part if total is None else total + part
        out = nt(e.astype(BF), pieces[p][0:KVR, :])
        acc = out if acc is None else acc + out
    if not first:
        alpha = jnp.exp2(m_prev - m_new)
        total = total + l_in[:, 0:1] * alpha
        acc = acc + acc_in[...] * alpha
    if mode == "state":
        acc_out, m_out, l_out = outs
        acc_out[...] = acc
        m_out[...] = jnp.broadcast_to(m_new, m_out.shape)
        l_out[...] = jnp.broadcast_to(total, l_out.shape)
        return
    norm = acc / total
    lse = m_new + jnp.log(total) * LOG2E
    if mode == "own":
        o_out, lse_out = outs
        o_out[...] = norm
        lse_out[...] = jnp.broadcast_to(lse, lse_out.shape)
        return
    (wire_out,) = outs
    wire_out[0:ROWS, :] = norm.astype(BF)
    diag = iota((ROWS, ROWS), 0) == iota((ROWS, ROWS), 1)
    row = jnp.sum(jnp.where(diag, lse, 0.0), axis=0, keepdims=True)
    hi, mid, lo = [x.astype(F32) for x in split3(row)]
    which = iota((16, ROWS), 0)
    left = jnp.where(which == 0, hi, jnp.where(which == 1, lo, 0.0))
    right = jnp.where(which == 0, mid, 0.0)
    wire_out[ROWS : ROWS + 16, 0:ROWS] = left.astype(BF)
    wire_out[ROWS : ROWS + 16, ROWS : 2 * ROWS] = right.astype(BF)


def score_kernel(count, *refs):
    pairs, keys, outs = refs[:count], refs[count : count + 4], refs[count + 4 :]
    me = lax.axis_index("ctx")
    unit = eye(IH)
    for pair, out in zip(pairs, outs):
        starts = (0, I_ROWS)
        both = jnp.concatenate([pair[k : k + I_W, :] for k in starts], axis=0)
        w_cols = [nt(unit, pair[k + I_W : k + I_ROWS, 0:IH]) for k in starts]
        for p in range(4):
            raw = jnp.maximum(nt(both, keys[p][0:TOK, :]), 0.0)
            scales = keys[p][TOK:K_ROWS, :].astype(F32)
            scale = jnp.concatenate([scales[c : c + 1, :] for c in range(CHUNKS)], axis=1)
            at = pl.multiple_of(lax.bitwise_and(lax.bitwise_xor(me, p), 3) * TOK, TOK)
            for side in range(2):
                for t in range(2):
                    row = side * 2 + t
                    weighted = raw[row * IH : (row + 1) * IH, :] * w_cols[side][:, t : t + 1]
                    line = jnp.sum(weighted, axis=0, keepdims=True) * scale
                    out[row : row + 1, pl.ds(at, TOK)] = line


def order_kernel(half_size, masks, *refs):
    me = lax.axis_index("ctx")
    own_ref, far_ref = refs[-2:]
    span = 4 * TOK
    for ref, mask in zip(refs, masks):
        at = lax.bitwise_and(lax.bitwise_xor(me, mask), half_size - 1) // 4 * span
        at = pl.multiple_of(at, span)
        own_ref[:, pl.ds(at, span)] = ref[0:2, :]
        far_ref[:, pl.ds(at, span)] = ref[2:4, :]


def halves_kernel(half_size, own_ref, far_ref, out_ref):
    half = lax.axis_index("ctx") // half_size
    width = half_size * TOK
    out_ref[:, pl.ds(pl.multiple_of(half * width, width), width)] = own_ref[...]
    out_ref[:, pl.ds(pl.multiple_of((1 - half) * width, width), width)] = far_ref[...]


def final_kernel(o_ref, lse_ref, wire_ref, out_ref):
    stats = wire_ref[ROWS : ROWS + 16, :].astype(F32)
    row = stats[0:1, 0:ROWS] + stats[0:1, ROWS : 2 * ROWS] + stats[1:2, 0:ROWS]
    diag = iota((ROWS, ROWS), 0) == iota((ROWS, ROWS), 1)
    lse_r = jnp.sum(jnp.where(diag, row, 0.0), axis=1, keepdims=True)
    lse_o = lse_ref[:, 0:1]
    top = jnp.maximum(lse_r, lse_o)
    e_r = jnp.exp2(lse_r - top)
    e_o = jnp.exp2(lse_o - top)
    inv = 1.0 / (e_r + e_o)
    out = o_ref[...] * (e_o * inv) + wire_ref[0:ROWS, :].astype(F32) * (e_r * inv)
    for t in range(2):
        out_ref[t] = out[t * HEADS : (t + 1) * HEADS, :].astype(BF)


def call(kernel, out_shape, name, flops, *args, scratch=(), specs=None, limit=48 << 20):
    moved = sum(a.size * a.dtype.itemsize for a in args)
    return pl.pallas_call(
        kernel,
        out_shape=out_shape,
        in_specs=specs or [VMEM] * len(args),
        out_specs=jax.tree.map(lambda _: VMEM, out_shape),
        scratch_shapes=list(scratch),
        name=name,
        cost_estimate=pl.CostEstimate(flops=int(flops), bytes_accessed=moved, transcendentals=0),
        compiler_params=pltpu.CompilerParams(vmem_limit_bytes=limit),
    )(*args)


def shape(dims, dtype):
    return jax.ShapeDtypeStruct(dims, dtype)


def attend(half_size, q, bias, group, state, mode, name):
    masks = tuple(mask for _, mask in group)
    args = [q, bias] + [piece for piece, _ in group]
    state_shape = (shape((ROWS, KVR), F32), shape((ROWS, 128), F32), shape((ROWS, 128), F32))
    if state is not None:
        args += list(state)
    if mode == "state":
        outs = state_shape
    elif mode == "wire":
        outs = shape((ROWS + 16, LANES), BF)
    else:
        outs = state_shape[:2]
    scratch = [pltpu.VMEM((ROWS, TOK * len(group)), F32)]
    flops = 2 * ROWS * TOK * len(group) * (2 * KVR + ROPE)
    return call(
        functools.partial(attend_kernel, half_size, masks, state is None, mode),
        outs,
        name,
        flops,
        *args,
        scratch=scratch,
    )


def local(n, index_queries, index_weights, index_keys, key_scales, q_latent, latents, wanted, selected):
    half_size = n // 2
    bits = n.bit_length() - 1
    top = 1 << (bits - 1)

    def permute(x, move):
        return lax.ppermute(x, "ctx", [(i, move(i)) for i in range(n)])

    def swap(x):
        return permute(x, lambda i: i ^ 1)

    def first(i):
        return i ^ 2 if i % 2 == 0 else i ^ 4

    def second(i):
        return i ^ 4 if i % 2 == 0 else i ^ 2

    kv = latents.T
    r1 = permute(kv, first)

    rows = 2 * half_size
    q_wire, bias_own, k_wire, kv_here = call(
        functools.partial(pack_kernel, half_size),
        (
            shape((Q_BIAS + CHUNKS * rows, 128), BF),
            shape((CHUNKS * rows, 128), BF),
            shape((K_ROWS, IDX), BF),
            shape((WIDTH, TOK), BF),
        ),
        "pack",
        2 * 2 * n * 4 * 2048 * 64,
        jnp.swapaxes(q_latent, 1, 2).reshape(2 * WIDTH, HEADS),
        index_queries.reshape(2 * IH, IDX),
        index_weights,
        index_keys,
        key_scales.reshape(CHUNKS, 128),
        selected,
        wanted[0].T,
        kv,
        specs=[HBM] * 8,
        limit=None,
        scratch=[
            pltpu.VMEM((2, IH), BF),
            pltpu.VMEM((CHUNKS, 128), BF),
            pltpu.VMEM(selected.shape, jnp.int32),
            pltpu.VMEM((wanted.shape[2], n), jnp.int32),
            pltpu.VMEM((2, n, LANES), F32),
            pltpu.SemaphoreType.DMA((8,)),
        ],
    )
    q_far = permute(q_wire, lambda i: i ^ top)
    r2 = permute(kv, second)
    q_far, r2 = lax.optimization_barrier((q_far, r2))
    r3 = permute(r1, second)
    held = [(kv_here, (0, 0)), (r1, (2, 4)), (r2, (4, 2)), (r3, (6, 6))]
    for bit in range(3, bits - 1):
        step = 1 << bit
        held = held + [
            (permute(piece, lambda i: i ^ step), (a ^ step, b ^ step)) for piece, (a, b) in held
        ]

    k_next = permute(k_wire, lambda i: i ^ 2)
    keys = [k_wire, swap(k_wire), k_next, swap(k_next)]

    def unpack(wire, bias, name, flops, more=()):
        return call(
            functools.partial(unpack_kernel, half_size),
            (shape((ROWS, WIDTH), BF), shape((rows, TOK), F32), *more),
            name,
            flops,
            q_wire,
            wire,
            bias,
        )

    q_far, *keys = lax.optimization_barrier((q_far, *keys))
    q_there, bias_there, i_pair = unpack(
        q_far, q_far, "unpack_far", 3 * 1.15e9, [shape((2 * I_ROWS, IDX), BF)]
    )
    i_pairs = [i_pair]
    for bit in range(2, bits - 1):
        step = 1 << bit
        i_pairs = i_pairs + [permute(x, lambda i: i ^ step) for x in i_pairs]
    q_here, bias_here = unpack(q_wire, bias_own, "unpack_own", 0)

    def pair(item):
        piece, (a, b) = item
        return [item, (swap(piece), (1 ^ b, 1 ^ a))]

    def run(q, bias, groups, last, name, state=None):
        for k, group in enumerate(groups):
            mode = last if k == len(groups) - 1 else "state"
            state = attend(half_size, q, bias, group, state, mode, f"{name}_{k}")
        return state

    near = [pair(item) for item in held[:3]]
    (own0, own1), (r1a, r1b), (r2a, r2b) = near
    far = attend(half_size, q_there, bias_there, [own0, own1, r1a, r2a], None, "state", "far_early")
    far, r3, *i_pairs = lax.optimization_barrier((far, r3, *i_pairs))
    held[3] = (r3, held[3][1])
    late = [pair(item) for item in held[3:]]
    rest = sum(late[1:], [])
    groups = [[r1b, r2b, late[0][0]], [late[0][1]]]
    groups += [rest[at : at + 6] for at in range(0, len(rest), 6)]
    wire = run(q_there, bias_there, groups, "wire", "far_late", far)
    o_far = permute(wire, lambda i: i ^ top)

    parts = call(
        functools.partial(score_kernel, len(i_pairs)),
        tuple(shape((4, 4 * TOK), F32) for _ in i_pairs),
        "index_scores",
        2 * len(i_pairs) * 4 * IH * 4 * TOK * IDX,
        *i_pairs,
        *keys,
    )
    parts = [[(part, 0)] for part in parts]
    for bit in reversed(range(2, bits - 1)):
        step = 1 << bit
        count = len(parts) // 2
        parts = [
            parts[j] + [(permute(x, lambda i: i ^ step), mask ^ step) for x, mask in parts[j + count]]
            for j in range(count)
        ]
    ranges = parts[0]
    scores_own, scores_far = call(
        functools.partial(order_kernel, half_size, tuple(mask for _, mask in ranges)),
        (shape((2, half_size * TOK), F32), shape((2, half_size * TOK), F32)),
        "order_scores",
        0,
        *[x for x, _ in ranges],
    )
    scores_far = permute(scores_far, lambda i: i ^ top)
    late = [sum(near + late[:1], [])] + groups[2:]
    o_own, lse_own = run(q_here, bias_here, late, "own", "own_late")
    attended = call(
        final_kernel,
        shape((2, HEADS, KVR), BF),
        "combine",
        10 * 1.15e9,
        o_own,
        lse_own,
        o_far,
    )
    attended, scores_far = lax.optimization_barrier((attended, scores_far))
    scores = call(
        functools.partial(halves_kernel, half_size),
        shape((2, n * TOK), F32),
        "join_scores",
        0,
        scores_own,
        scores_far,
    )
    return scores, attended


def solution(mesh):
    spec = P(("groups", "ctx"))
    return jax.shard_map(
        functools.partial(local, mesh.shape["ctx"]),
        mesh=mesh,
        in_specs=(spec,) * 8,
        out_specs=(spec, spec),
        check_vma=False,
    )
```

```python
import functools

import jax
import jax.numpy as jnp
from jax import lax
from jax.experimental import pallas as pl
from jax.experimental.pallas import tpu as pltpu
from jax.sharding import PartitionSpec as P

BLOCK = 64
LANES = 512
KVR = 512
ROPE = 64
HEADS = 128
IH = 32
IDX = 128
TOK = 512
NEG = -1e30
LOG2E = 1.4426950408889634
TO_LOG2 = 192.0 ** (-0.5) * LOG2E

WIDTH = KVR + ROPE
ROWS = 2 * HEADS
CHUNKS = TOK // 128

I_W = 2 * IH
I_ROWS = I_W + 16
K_ROWS = TOK + 16

Q_IDX = 2 * WIDTH
Q_BIAS = Q_IDX + I_ROWS

BF = jnp.bfloat16
F32 = jnp.float32
VMEM = pl.BlockSpec(memory_space=pltpu.VMEM)
HBM = pl.BlockSpec(memory_space=pltpu.HBM)


def nn(a, b):
    return lax.dot_general(a, b, (((1,), (0,)), ((), ())), preferred_element_type=F32)


def nt(a, b):
    return lax.dot_general(a, b, (((1,), (1,)), ((), ())), preferred_element_type=F32)


def iota(shape, dim):
    return lax.broadcasted_iota(jnp.int32, shape, dim)


def onehot(cond):
    return jnp.where(cond, 1.0, 0.0).astype(BF)


def eye(n):
    return onehot(iota((n, n), 0) == iota((n, n), 1))


def pack_kernel(
    half_size, q_in, iq_in, w_in, keys_in, scale_in, sel_in, want_in,
    wire_ref, own_ref, k_ref, i_ref, w_ref, scale_ref, sel_ref, want_ref, bias, sems,
):
    moves = [
        (sel_in, sel_ref),
        (want_in, want_ref),
        (w_in, w_ref),
        (scale_in, scale_ref),
        (q_in, wire_ref.at[0:Q_IDX]),
        (iq_in, wire_ref.at[Q_IDX : Q_IDX + I_W]),
        (keys_in, k_ref.at[0:TOK]),
        (iq_in, i_ref.at[0:I_W]),
    ]
    copies = [
        pltpu.make_async_copy(src, dst, sems.at[k]) for k, (src, dst) in enumerate(moves)
    ]
    for copy in copies:
        copy.start()
    wire_ref[Q_IDX + I_W : Q_BIAS, :] = jnp.zeros((16, IDX), BF)
    i_ref[I_W:I_ROWS, :] = jnp.zeros((16, IDX), BF)
    k_ref[TOK:K_ROWS, :] = jnp.zeros((16, IDX), BF)
    for copy in copies[:4]:
        copy.wait()
    wire_ref[Q_IDX + I_W : Q_IDX + I_W + 2, 0:IH] = w_ref[...]
    i_ref[I_W : I_W + 2, 0:IH] = w_ref[...]
    k_ref[TOK : TOK + CHUNKS, :] = scale_ref[...]
    me = lax.axis_index("ctx")
    half = me // half_size
    n = 2 * half_size
    slots = want_ref.shape[0]
    topk = sel_ref.shape[1]
    asked = nt(eye(n), want_ref[...].astype(F32).astype(BF))
    lane_block = (iota((n, LANES), 1) // BLOCK).astype(F32)
    spread = onehot(iota((BLOCK, LANES), 1) % BLOCK == iota((BLOCK, LANES), 0))
    line = iota((slots * n, topk), 0)
    slot_of_line = (line % n) * slots + line // n
    for t in range(2):
        sel = sel_ref[t : t + 1, :]
        inner = onehot(sel % BLOCK == iota((BLOCK, topk), 0))
        count = nt(onehot(sel // BLOCK == slot_of_line), inner)
        wide = nn(count.astype(BF), spread)
        total = jnp.zeros((n, LANES), F32)
        for b in range(slots):
            total = total + jnp.where(
                lane_block == asked[:, b : b + 1], wide[b * n : (b + 1) * n, :], 0.0
            )
        bias[t] = jnp.where(total > 0.5, 0.0, NEG)
    mine = pl.multiple_of(half * half_size, half_size)
    other = pl.multiple_of((1 - half) * half_size, half_size)
    rows = 2 * half_size
    for c in range(CHUNKS):
        lanes = slice(c * 128, (c + 1) * 128)
        own_ref[c * rows : (c + 1) * rows, :] = jnp.concatenate(
            [bias[t, pl.ds(mine, half_size), lanes] for t in range(2)], axis=0
        ).astype(BF)
        wire_ref[Q_BIAS + c * rows : Q_BIAS + (c + 1) * rows, :] = jnp.concatenate(
            [bias[t, pl.ds(other, half_size), lanes] for t in range(2)], axis=0
        ).astype(BF)
    for copy in copies[4:]:
        copy.wait()


def stage_kernel(kv_in, i_in, kv_ref, i_ref, sems):
    copies = [
        pltpu.make_async_copy(kv_in, kv_ref, sems.at[0]),
        pltpu.make_async_copy(i_in, i_ref, sems.at[1]),
    ]
    for copy in copies:
        copy.start()
    for copy in copies:
        copy.wait()


def unpack_kernel(half_size, *refs):
    if len(refs) == 6:
        wire_ref, bias_ref, own_ref, q_ref, out_ref, pair_ref = refs
        pair_ref[0:I_ROWS, :] = own_ref[...]
        pair_ref[I_ROWS : 2 * I_ROWS, :] = wire_ref[Q_IDX:Q_BIAS, :]
    else:
        wire_ref, bias_ref, q_ref, out_ref = refs
    for t in range(2):
        rows = nt(eye(HEADS), wire_ref[t * WIDTH : (t + 1) * WIDTH, :])
        q_ref[t * HEADS : (t + 1) * HEADS, :] = rows.astype(BF)
    rows = 2 * half_size
    base = bias_ref.shape[0] - CHUNKS * rows
    for c in range(CHUNKS):
        out_ref[:, c * 128 : (c + 1) * 128] = bias_ref[
            base + c * rows : base + (c + 1) * rows, :
        ].astype(F32)


def attend_kernel(half_size, masks, first, mode, queries, *refs):
    count = len(masks)
    refs = list(refs)
    q_ref, bias_ref = refs[:2]
    pieces = refs[2 : 2 + count]
    pos = 2 + count
    if not first:
        acc_in, m_in, l_in = refs[pos : pos + 3]
        pos += 3
    outs = refs[pos:-1]
    logits = refs[-1]

    me = lax.axis_index("ctx")
    core = me % 2
    span = slice(queries[0] * HEADS, (queries[-1] + 1) * HEADS)
    size = len(queries) * HEADS
    q = q_ref[span, :]
    m_prev = None if first else m_in[span, 0:1]
    m_new = m_prev
    for p in range(count):
        kv = pieces[p]
        src = lax.bitwise_xor(me, jnp.where(core == 0, masks[p][0], masks[p][1]))
        src = src % half_size
        s = nn(q, kv[0:WIDTH, :]) * TO_LOG2
        for k, t in enumerate(queries):
            part = s[k * HEADS : (k + 1) * HEADS, :] + bias_ref[pl.ds(t * half_size + src, 1), :]
            logits[k * HEADS : (k + 1) * HEADS, p * TOK : (p + 1) * TOK] = part
    top = jnp.max(logits[...], axis=1, keepdims=True)
    m_new = top if first else jnp.maximum(m_prev, top)

    total = None
    acc = None
    for p in range(count):
        e = jnp.exp2(logits[:, p * TOK : (p + 1) * TOK] - m_new)
        part = jnp.sum(e, axis=1, keepdims=True)
        total = part if total is None else total + part
        out = nt(e.astype(BF), pieces[p][0:KVR, :])
        acc = out if acc is None else acc + out
    if not first:
        alpha = jnp.exp2(m_prev - m_new)
        total = total + l_in[span, 0:1] * alpha
        acc = acc + acc_in[span, :] * alpha
    if mode == "state":
        acc_out, m_out, l_out = outs
        acc_out[...] = acc
        m_out[...] = jnp.broadcast_to(m_new, m_out.shape)
        l_out[...] = jnp.broadcast_to(total, l_out.shape)
        return
    norm = acc / total
    lse = m_new + jnp.log(total) * LOG2E
    if mode == "own":
        o_out, lse_out = outs
        o_out[...] = norm
        lse_out[...] = jnp.broadcast_to(lse, lse_out.shape)
        return
    wire_out, lse_out = outs
    wire_out[...] = norm.astype(BF)
    diag = iota((HEADS, HEADS), 0) == iota((HEADS, HEADS), 1)
    for t in range(2):
        column = lse[t * HEADS : (t + 1) * HEADS, :]
        lse_out[t : t + 1, :] = jnp.sum(jnp.where(diag, column, 0.0), axis=0, keepdims=True)


def pairs_kernel(*refs):
    pairs, outs = refs[: len(refs) // 3], refs[len(refs) // 3 :]
    for j, pair in enumerate(pairs):
        q_ref, w_ref = outs[2 * j : 2 * j + 2]
        for k in range(2):
            at = k * I_ROWS
            q_ref[k * I_W : (k + 1) * I_W, :] = pair[at : at + I_W, :]
            w_ref[k] = nt(eye(IH), pair[at + I_W : at + I_ROWS, 0:IH])


def score_kernel(count, *refs):
    pairs, refs = refs[: 2 * count], refs[2 * count :]
    keys, outs = refs[:4], refs[4:]
    me = lax.axis_index("ctx")
    for j, out in enumerate(outs):
        both = pairs[2 * j][...]
        w_cols = [pairs[2 * j + 1][k] for k in range(2)]
        for p in range(4):
            raw = jnp.maximum(nt(both, keys[p][0:TOK, :]), 0.0)
            scales = keys[p][TOK:K_ROWS, :].astype(F32)
            scale = jnp.concatenate([scales[c : c + 1, :] for c in range(CHUNKS)], axis=1)
            at = pl.multiple_of(lax.bitwise_and(lax.bitwise_xor(me, p), 3) * TOK, TOK)
            for side in range(2):
                for t in range(2):
                    row = side * 2 + t
                    weighted = raw[row * IH : (row + 1) * IH, :] * w_cols[side][:, t : t + 1]
                    line = jnp.sum(weighted, axis=0, keepdims=True) * scale
                    out[row : row + 1, pl.ds(at, TOK)] = line


def order_kernel(half_size, masks, *refs):
    me = lax.axis_index("ctx")
    lse_ref, own_ref, far_ref = refs[-3:]
    span = 4 * TOK
    far_ref[:, half_size * TOK :] = lse_ref[...]
    for ref, mask in zip(refs, masks):
        at = lax.bitwise_and(lax.bitwise_xor(me, mask), half_size - 1) // 4 * span
        at = pl.multiple_of(at, span)
        own_ref[:, pl.ds(at, span)] = ref[0:2, :]
        far_ref[:, pl.ds(at, span)] = ref[2:4, :]


def finish_kernel(half_size, o_ref, lse_ref, wire_ref, own_ref, far_ref, scores_ref, out_ref):
    half = lax.axis_index("ctx") // half_size
    width = half_size * TOK
    scores_ref[:, pl.ds(pl.multiple_of(half * width, width), width)] = own_ref[...]
    scores_ref[:, pl.ds(pl.multiple_of((1 - half) * width, width), width)] = far_ref[:, 0:width]
    diag = iota((HEADS, HEADS), 0) == iota((HEADS, HEADS), 1)
    lse_r = jnp.concatenate(
        [
            jnp.sum(jnp.where(diag, far_ref[t : t + 1, width:], 0.0), axis=1, keepdims=True)
            for t in range(2)
        ],
        axis=0,
    )
    lse_o = lse_ref[:, 0:1]
    top = jnp.maximum(lse_r, lse_o)
    e_r = jnp.exp2(lse_r - top)
    e_o = jnp.exp2(lse_o - top)
    inv = 1.0 / (e_r + e_o)
    out = o_ref[...] * (e_o * inv) + wire_ref[...].astype(F32) * (e_r * inv)
    for t in range(2):
        out_ref[t] = out[t * HEADS : (t + 1) * HEADS, :].astype(BF)


def call(kernel, out_shape, name, flops, *args, scratch=(), specs=None, limit=48 << 20):
    moved = sum(a.size * a.dtype.itemsize for a in args)
    return pl.pallas_call(
        kernel,
        out_shape=out_shape,
        in_specs=specs or [VMEM] * len(args),
        out_specs=jax.tree.map(lambda _: VMEM, out_shape),
        scratch_shapes=list(scratch),
        name=name,
        cost_estimate=pl.CostEstimate(flops=int(flops), bytes_accessed=moved, transcendentals=0),
        compiler_params=pltpu.CompilerParams(vmem_limit_bytes=limit),
    )(*args)


def shape(dims, dtype):
    return jax.ShapeDtypeStruct(dims, dtype)


def attend(half_size, q, bias, group, state, mode, name, queries=(0, 1)):
    masks = tuple(mask for _, mask in group)
    args = [q, bias] + [piece for piece, _ in group]
    size = len(queries) * HEADS
    state_shape = (shape((ROWS, KVR), F32), shape((ROWS, 128), F32), shape((ROWS, 128), F32))
    if state is not None:
        args += list(state)
    if mode == "state":
        outs = state_shape
    elif mode == "wire":
        outs = (shape((ROWS, KVR), BF), shape((2, HEADS), F32))
    else:
        outs = state_shape[:2]
    scratch = [pltpu.VMEM((size, TOK * len(group)), F32)]
    flops = 2 * size * TOK * len(group) * (2 * KVR + ROPE)
    return call(
        functools.partial(attend_kernel, half_size, masks, state is None, mode, queries),
        outs,
        name,
        flops,
        *args,
        scratch=scratch,
    )


def local(n, index_queries, index_weights, index_keys, key_scales, q_latent, latents, wanted, selected):
    half_size = n // 2
    bits = n.bit_length() - 1
    top = 1 << (bits - 1)

    def permute(x, move):
        return lax.ppermute(x, "ctx", [(i, move(i)) for i in range(n)])

    def swap(x):
        return permute(x, lambda i: i ^ 1)

    def first(i):
        return i ^ 2 if i % 2 == 0 else i ^ 4

    def second(i):
        return i ^ 4 if i % 2 == 0 else i ^ 2

    kv = latents.T
    r1 = permute(kv, first)

    rows = 2 * half_size
    q_wire, bias_own, k_wire, i_own = call(
        functools.partial(pack_kernel, half_size),
        (
            shape((Q_BIAS + CHUNKS * rows, 128), BF),
            shape((CHUNKS * rows, 128), BF),
            shape((K_ROWS, IDX), BF),
            shape((I_ROWS, IDX), BF),
        ),
        "pack",
        2 * 2 * n * 4 * 2048 * 64,
        jnp.swapaxes(q_latent, 1, 2).reshape(2 * WIDTH, HEADS),
        index_queries.reshape(2 * IH, IDX),
        index_weights,
        index_keys,
        key_scales.reshape(CHUNKS, 128),
        selected,
        wanted[0].T,
        specs=[HBM] * 7,
        limit=None,
        scratch=[
            pltpu.VMEM((2, IH), BF),
            pltpu.VMEM((CHUNKS, 128), BF),
            pltpu.VMEM(selected.shape, jnp.int32),
            pltpu.VMEM((wanted.shape[2], n), jnp.int32),
            pltpu.VMEM((2, n, LANES), F32),
            pltpu.SemaphoreType.DMA((8,)),
        ],
    )
    kv, q_wire = lax.optimization_barrier((kv, q_wire))
    q_far = permute(q_wire, lambda i: i ^ top)
    r2 = permute(kv, second)
    q_far, r2 = lax.optimization_barrier((q_far, r2))
    r3 = permute(r1, second)
    held = [(kv, (0, 0)), (r1, (2, 4)), (r2, (4, 2)), (r3, (6, 6))]
    for bit in range(3, bits - 1):
        step = 1 << bit
        held = held + [
            (permute(piece, lambda i: i ^ step), (a ^ step, b ^ step)) for piece, (a, b) in held
        ]

    k_next = permute(k_wire, lambda i: i ^ 2)
    kv_here, i_own = call(
        stage_kernel,
        (shape((WIDTH, TOK), BF), shape((I_ROWS, IDX), BF)),
        "stage",
        0,
        kv,
        i_own,
        specs=[HBM] * 2,
        scratch=[pltpu.SemaphoreType.DMA((2,))],
    )
    kv_core = swap(kv_here)
    k_next, kv_core = lax.optimization_barrier((k_next, kv_core))
    keys = [k_wire, swap(k_wire), k_next, swap(k_next)]

    def unpack(name, flops, *args):
        outs = [shape((ROWS, WIDTH), BF), shape((rows, TOK), F32)]
        if len(args) == 3:
            outs.append(shape((2 * I_ROWS, IDX), BF))
        return call(functools.partial(unpack_kernel, half_size), tuple(outs), name, flops, *args)

    q_far, *keys = lax.optimization_barrier((q_far, *keys))
    q_there, bias_there, i_pair = unpack("unpack_far", 3 * 1.15e9, q_far, q_far, i_own)
    q_here, bias_here = unpack("unpack_own", 0, q_wire, bias_own)

    def pair(item):
        piece, (a, b) = item
        return [item, (swap(piece), (1 ^ b, 1 ^ a))]

    def run(q, bias, groups, last, name, state=None):
        for k, group in enumerate(groups):
            mode = last if k == len(groups) - 1 else "state"
            state = attend(half_size, q, bias, group, state, mode, f"{name}_{k}")
        return state

    near = [[(kv_here, (0, 0)), (kv_core, (1, 1))]] + [pair(item) for item in held[1:3]]
    (own0, own1), (r1a, r1b), (r2a, r2b) = near
    far = attend(half_size, q_there, bias_there, [own0, own1, r1a, r2a], None, "state", "far_early")
    i_pairs = [i_pair]
    for bit in range(2, bits - 1):
        step = 1 << bit
        i_pairs = i_pairs + [permute(x, lambda i: i ^ step) for x in i_pairs]
    far, r3 = lax.optimization_barrier((far, r3))
    held[3] = (r3, held[3][1])
    late = [pair(item) for item in held[3:]]
    rest = sum(late[1:], [])
    groups = [[r1b, r2b, late[0][0]], [late[0][1]]]
    groups += [rest[at : at + 6] for at in range(0, len(rest), 6)]
    far = run(q_there, bias_there, groups[:-1], "state", "far_late", far)
    prepared = call(
        pairs_kernel,
        (shape((2 * I_W, IDX), BF), shape((2, IH, 16), F32)) * len(i_pairs),
        "index_pairs",
        6 * 1.15e9,
        *i_pairs,
    )
    *far, prepared = lax.optimization_barrier((*far, prepared))
    wire = attend(half_size, q_there, bias_there, groups[-1], far, "wire", "far_last")
    wire, lse_far = wire
    o_far = permute(wire, lambda i: i ^ top)

    parts = call(
        functools.partial(score_kernel, len(i_pairs)),
        tuple(shape((4, 4 * TOK), F32) for _ in i_pairs),
        "index_scores",
        2 * len(i_pairs) * 4 * IH * 4 * TOK * IDX,
        *prepared,
        *keys,
    )
    parts = [[(part, 0)] for part in parts]
    for bit in reversed(range(2, bits - 1)):
        step = 1 << bit
        count = len(parts) // 2
        parts = [
            parts[j] + [(permute(x, lambda i: i ^ step), mask ^ step) for x, mask in parts[j + count]]
            for j in range(count)
        ]
    late = [sum(near + late[:1], [])] + groups[2:]
    o_own, lse_own = run(q_here, bias_here, late, "own", "own_late")
    ranges, o_own = lax.optimization_barrier((parts[0], o_own))
    scores_own, scores_far = call(
        functools.partial(order_kernel, half_size, tuple(mask for _, mask in parts[0])),
        (shape((2, half_size * TOK), F32), shape((2, half_size * TOK + HEADS), F32)),
        "order_scores",
        0,
        *[x for x, _ in ranges],
        lse_far,
    )
    scores_far = permute(scores_far, lambda i: i ^ top)

    return call(
        functools.partial(finish_kernel, half_size),
        (shape((2, n * TOK), F32), shape((2, HEADS, KVR), BF)),
        "finish",
        ROWS * KVR * 4,
        o_own,
        lse_own,
        o_far,
        scores_own,
        scores_far,
    )


def solution(mesh):
    spec = P(("groups", "ctx"))
    return jax.shard_map(
        functools.partial(local, mesh.shape["ctx"]),
        mesh=mesh,
        in_specs=(spec,) * 8,
        out_specs=(spec, spec),
        check_vma=False,
    )
```

```python
import functools

import jax
import jax.numpy as jnp
from jax import lax
from jax.experimental import pallas as pl
from jax.experimental.pallas import tpu as pltpu
from jax.sharding import PartitionSpec as P

BLOCK = 64
LANES = 512
KVR = 512
ROPE = 64
HEADS = 128
IH = 32
IDX = 128
TOK = 512
NEG = -1e30
LOG2E = 1.4426950408889634
TO_LOG2 = 192.0 ** (-0.5) * LOG2E

WIDTH = KVR + ROPE
ROWS = 2 * HEADS
CHUNKS = TOK // 128

I_W = 2 * IH
I_ROWS = I_W + 16
K_ROWS = TOK + 16

Q_IDX = 2 * WIDTH
Q_BIAS = Q_IDX + I_ROWS

BF = jnp.bfloat16
F32 = jnp.float32
VMEM = pl.BlockSpec(memory_space=pltpu.VMEM)
HBM = pl.BlockSpec(memory_space=pltpu.HBM)


def nn(a, b):
    return lax.dot_general(a, b, (((1,), (0,)), ((), ())), preferred_element_type=F32)


def nt(a, b):
    return lax.dot_general(a, b, (((1,), (1,)), ((), ())), preferred_element_type=F32)


def iota(shape, dim):
    return lax.broadcasted_iota(jnp.int32, shape, dim)


def onehot(cond):
    return jnp.where(cond, 1.0, 0.0).astype(BF)


def eye(n):
    return onehot(iota((n, n), 0) == iota((n, n), 1))


def pack_kernel(
    half_size, q_in, iq_in, w_in, keys_in, scale_in, sel_in, want_in,
    wire_ref, own_ref, k_ref, i_ref, w_ref, scale_ref, sel_ref, want_ref, bias, sems,
):
    moves = [
        (sel_in, sel_ref),
        (want_in, want_ref),
        (w_in, w_ref),
        (scale_in, scale_ref),
        (q_in, wire_ref.at[0:Q_IDX]),
        (iq_in, wire_ref.at[Q_IDX : Q_IDX + I_W]),
        (keys_in, k_ref.at[0:TOK]),
        (iq_in, i_ref.at[0:I_W]),
    ]
    copies = [
        pltpu.make_async_copy(src, dst, sems.at[k]) for k, (src, dst) in enumerate(moves)
    ]
    for copy in copies:
        copy.start()
    wire_ref[Q_IDX + I_W : Q_BIAS, :] = jnp.zeros((16, IDX), BF)
    i_ref[I_W:I_ROWS, :] = jnp.zeros((16, IDX), BF)
    k_ref[TOK:K_ROWS, :] = jnp.zeros((16, IDX), BF)
    for copy in copies[:4]:
        copy.wait()
    wire_ref[Q_IDX + I_W : Q_IDX + I_W + 2, 0:IH] = w_ref[...]
    i_ref[I_W : I_W + 2, 0:IH] = w_ref[...]
    k_ref[TOK : TOK + CHUNKS, :] = scale_ref[...]
    me = lax.axis_index("ctx")
    half = me // half_size
    n = 2 * half_size
    slots = want_ref.shape[0]
    topk = sel_ref.shape[1]
    asked = nt(eye(n), want_ref[...].astype(F32).astype(BF))
    lane_block = (iota((n, LANES), 1) // BLOCK).astype(F32)
    spread = onehot(iota((BLOCK, LANES), 1) % BLOCK == iota((BLOCK, LANES), 0))
    line = iota((slots * n, topk), 0)
    slot_of_line = (line % n) * slots + line // n
    for t in range(2):
        sel = sel_ref[t : t + 1, :]
        inner = onehot(sel % BLOCK == iota((BLOCK, topk), 0))
        count = nt(onehot(sel // BLOCK == slot_of_line), inner)
        wide = nn(count.astype(BF), spread)
        total = jnp.zeros((n, LANES), F32)
        for b in range(slots):
            total = total + jnp.where(
                lane_block == asked[:, b : b + 1], wide[b * n : (b + 1) * n, :], 0.0
            )
        bias[t] = jnp.where(total > 0.5, 0.0, NEG)
    mine = pl.multiple_of(half * half_size, half_size)
    other = pl.multiple_of((1 - half) * half_size, half_size)
    rows = 2 * half_size
    for c in range(CHUNKS):
        lanes = slice(c * 128, (c + 1) * 128)
        own_ref[c * rows : (c + 1) * rows, :] = jnp.concatenate(
            [bias[t, pl.ds(mine, half_size), lanes] for t in range(2)], axis=0
        ).astype(BF)
        wire_ref[Q_BIAS + c * rows : Q_BIAS + (c + 1) * rows, :] = jnp.concatenate(
            [bias[t, pl.ds(other, half_size), lanes] for t in range(2)], axis=0
        ).astype(BF)
    for copy in copies[4:]:
        copy.wait()


def stage_kernel(kv_in, i_in, kv_ref, i_ref, sems):
    copies = [
        pltpu.make_async_copy(kv_in, kv_ref, sems.at[0]),
        pltpu.make_async_copy(i_in, i_ref, sems.at[1]),
    ]
    for copy in copies:
        copy.start()
    for copy in copies:
        copy.wait()


def unpack_kernel(half_size, *refs):
    if len(refs) == 6:
        wire_ref, bias_ref, own_ref, q_ref, out_ref, pair_ref = refs
        pair_ref[0:I_ROWS, :] = own_ref[...]
        pair_ref[I_ROWS : 2 * I_ROWS, :] = wire_ref[Q_IDX:Q_BIAS, :]
    else:
        wire_ref, bias_ref, q_ref, out_ref = refs
    for t in range(2):
        rows = nt(eye(HEADS), wire_ref[t * WIDTH : (t + 1) * WIDTH, :])
        q_ref[t * HEADS : (t + 1) * HEADS, :] = rows.astype(BF)
    rows = 2 * half_size
    base = bias_ref.shape[0] - CHUNKS * rows
    for c in range(CHUNKS):
        out_ref[:, c * 128 : (c + 1) * 128] = bias_ref[
            base + c * rows : base + (c + 1) * rows, :
        ].astype(F32)


def attend_kernel(half_size, masks, first, mode, queries, *refs):
    count = len(masks)
    refs = list(refs)
    q_ref, bias_ref = refs[:2]
    pieces = refs[2 : 2 + count]
    pos = 2 + count
    if not first:
        acc_in, m_in, l_in = refs[pos : pos + 3]
        pos += 3
    outs = refs[pos:-1]
    logits = refs[-1]

    me = lax.axis_index("ctx")
    core = me % 2
    span = slice(queries[0] * HEADS, (queries[-1] + 1) * HEADS)
    size = len(queries) * HEADS
    q = q_ref[span, :]
    m_prev = None if first else m_in[span, 0:1]
    m_new = m_prev
    for p in range(count):
        kv = pieces[p]
        src = lax.bitwise_xor(me, jnp.where(core == 0, masks[p][0], masks[p][1]))
        src = src % half_size
        s = nn(q, kv[0:WIDTH, :]) * TO_LOG2
        for k, t in enumerate(queries):
            part = s[k * HEADS : (k + 1) * HEADS, :] + bias_ref[pl.ds(t * half_size + src, 1), :]
            logits[k * HEADS : (k + 1) * HEADS, p * TOK : (p + 1) * TOK] = part
    top = jnp.max(logits[...], axis=1, keepdims=True)
    m_new = top if first else jnp.maximum(m_prev, top)

    total = None
    acc = None
    for p in range(count):
        e = jnp.exp2(logits[:, p * TOK : (p + 1) * TOK] - m_new)
        part = jnp.sum(e, axis=1, keepdims=True)
        total = part if total is None else total + part
        out = nt(e.astype(BF), pieces[p][0:KVR, :])
        acc = out if acc is None else acc + out
    if not first:
        alpha = jnp.exp2(m_prev - m_new)
        total = total + l_in[span, 0:1] * alpha
        acc = acc + acc_in[span, :] * alpha
    if mode == "state":
        acc_out, m_out, l_out = outs
        acc_out[...] = acc
        m_out[...] = jnp.broadcast_to(m_new, m_out.shape)
        l_out[...] = jnp.broadcast_to(total, l_out.shape)
        return
    norm = acc * (1.0 / total)
    lse = m_new + jnp.log(total) * LOG2E
    if mode == "own":
        o_out, lse_out = outs
        o_out[...] = norm
        lse_out[...] = jnp.broadcast_to(lse, lse_out.shape)
        return
    wire_out, lse_out = outs
    wire_out[...] = norm.astype(BF)
    diag = iota((HEADS, HEADS), 0) == iota((HEADS, HEADS), 1)
    for t in range(2):
        column = lse[t * HEADS : (t + 1) * HEADS, :]
        lse_out[t : t + 1, :] = jnp.sum(jnp.where(diag, column, 0.0), axis=0, keepdims=True)


def pairs_kernel(*refs):
    pairs, outs = refs[: len(refs) // 3], refs[len(refs) // 3 :]
    for j, pair in enumerate(pairs):
        q_ref, w_ref = outs[2 * j : 2 * j + 2]
        for k in range(2):
            at = k * I_ROWS
            q_ref[k * I_W : (k + 1) * I_W, :] = pair[at : at + I_W, :]
            w_ref[k] = nt(eye(IH), pair[at + I_W : at + I_ROWS, 0:IH])


def score_kernel(count, *refs):
    pairs, refs = refs[: 2 * count], refs[2 * count :]
    keys, outs = refs[:4], refs[4:]
    me = lax.axis_index("ctx")
    for j, out in enumerate(outs):
        both = pairs[2 * j][...]
        w_cols = [pairs[2 * j + 1][k] for k in range(2)]
        for p in range(4):
            raw = jnp.maximum(nt(both, keys[p][0:TOK, :]), 0.0)
            scales = keys[p][TOK:K_ROWS, :].astype(F32)
            scale = jnp.concatenate([scales[c : c + 1, :] for c in range(CHUNKS)], axis=1)
            at = pl.multiple_of(lax.bitwise_and(lax.bitwise_xor(me, p), 3) * TOK, TOK)
            for side in range(2):
                for t in range(2):
                    row = side * 2 + t
                    weighted = raw[row * IH : (row + 1) * IH, :] * w_cols[side][:, t : t + 1]
                    line = jnp.sum(weighted, axis=0, keepdims=True) * scale
                    out[row : row + 1, pl.ds(at, TOK)] = line


def order_kernel(half_size, masks, *refs):
    me = lax.axis_index("ctx")
    lse_ref, own_ref, far_ref = refs[-3:]
    span = 4 * TOK
    width = half_size * TOK
    hi = lse_ref[...].astype(BF)
    rest = lse_ref[...] - hi.astype(F32)
    mid = rest.astype(BF)
    parts = (hi, mid, (rest - mid.astype(F32)).astype(BF))
    for k, part in enumerate(parts):
        far_ref[:, width + k * HEADS : width + (k + 1) * HEADS] = part
    for ref, mask in zip(refs, masks):
        at = lax.bitwise_and(lax.bitwise_xor(me, mask), half_size - 1) // 4 * span
        at = pl.multiple_of(at, span)
        own_ref[:, pl.ds(at, span)] = ref[0:2, :]
        far_ref[:, pl.ds(at, span)] = ref[2:4, :].astype(BF)


def finish_kernel(half_size, o_ref, lse_ref, wire_ref, own_ref, far_ref, scores_ref, out_ref):
    half = lax.axis_index("ctx") // half_size
    width = half_size * TOK
    scores_ref[:, pl.ds(pl.multiple_of(half * width, width), width)] = own_ref[...]
    scores_ref[:, pl.ds(pl.multiple_of((1 - half) * width, width), width)] = far_ref[:, 0:width].astype(F32)
    stats = far_ref[:, width:].astype(F32)
    stats = stats[:, 0:HEADS] + stats[:, HEADS : 2 * HEADS] + stats[:, 2 * HEADS : 3 * HEADS]
    diag = iota((HEADS, HEADS), 0) == iota((HEADS, HEADS), 1)
    lse_r = jnp.concatenate(
        [
            jnp.sum(jnp.where(diag, stats[t : t + 1, :], 0.0), axis=1, keepdims=True)
            for t in range(2)
        ],
        axis=0,
    )
    lse_o = lse_ref[:, 0:1]
    top = jnp.maximum(lse_r, lse_o)
    e_r = jnp.exp2(lse_r - top)
    e_o = jnp.exp2(lse_o - top)
    inv = 1.0 / (e_r + e_o)
    out = o_ref[...] * (e_o * inv) + wire_ref[...].astype(F32) * (e_r * inv)
    for t in range(2):
        out_ref[t] = out[t * HEADS : (t + 1) * HEADS, :].astype(BF)


def call(kernel, out_shape, name, flops, *args, scratch=(), specs=None, limit=48 << 20):
    moved = sum(a.size * a.dtype.itemsize for a in args)
    return pl.pallas_call(
        kernel,
        out_shape=out_shape,
        in_specs=specs or [VMEM] * len(args),
        out_specs=jax.tree.map(lambda _: VMEM, out_shape),
        scratch_shapes=list(scratch),
        name=name,
        cost_estimate=pl.CostEstimate(flops=int(flops), bytes_accessed=moved, transcendentals=0),
        compiler_params=pltpu.CompilerParams(vmem_limit_bytes=limit),
    )(*args)


def shape(dims, dtype):
    return jax.ShapeDtypeStruct(dims, dtype)


def attend(half_size, q, bias, group, state, mode, name, queries=(0, 1)):
    masks = tuple(mask for _, mask in group)
    args = [q, bias] + [piece for piece, _ in group]
    size = len(queries) * HEADS
    state_shape = (shape((ROWS, KVR), F32), shape((ROWS, 128), F32), shape((ROWS, 128), F32))
    if state is not None:
        args += list(state)
    if mode == "state":
        outs = state_shape
    elif mode == "wire":
        outs = (shape((ROWS, KVR), BF), shape((2, HEADS), F32))
    else:
        outs = state_shape[:2]
    scratch = [pltpu.VMEM((size, TOK * len(group)), F32)]
    flops = 2 * size * TOK * len(group) * (2 * KVR + ROPE)
    return call(
        functools.partial(attend_kernel, half_size, masks, state is None, mode, queries),
        outs,
        name,
        flops,
        *args,
        scratch=scratch,
    )


def local(n, index_queries, index_weights, index_keys, key_scales, q_latent, latents, wanted, selected):
    half_size = n // 2
    bits = n.bit_length() - 1
    top = 1 << (bits - 1)

    def permute(x, move):
        return lax.ppermute(x, "ctx", [(i, move(i)) for i in range(n)])

    def swap(x):
        return permute(x, lambda i: i ^ 1)

    def first(i):
        return i ^ 2 if i % 2 == 0 else i ^ 4

    def second(i):
        return i ^ 4 if i % 2 == 0 else i ^ 2

    kv = latents.T
    r1 = permute(kv, first)

    rows = 2 * half_size
    q_wire, bias_own, k_wire, i_own = call(
        functools.partial(pack_kernel, half_size),
        (
            shape((Q_BIAS + CHUNKS * rows, 128), BF),
            shape((CHUNKS * rows, 128), BF),
            shape((K_ROWS, IDX), BF),
            shape((I_ROWS, IDX), BF),
        ),
        "pack",
        2 * 2 * n * 4 * 2048 * 64,
        jnp.swapaxes(q_latent, 1, 2).reshape(2 * WIDTH, HEADS),
        index_queries.reshape(2 * IH, IDX),
        index_weights,
        index_keys,
        key_scales.reshape(CHUNKS, 128),
        selected,
        wanted[0].T,
        specs=[HBM] * 7,
        limit=None,
        scratch=[
            pltpu.VMEM((2, IH), BF),
            pltpu.VMEM((CHUNKS, 128), BF),
            pltpu.VMEM(selected.shape, jnp.int32),
            pltpu.VMEM((wanted.shape[2], n), jnp.int32),
            pltpu.VMEM((2, n, LANES), F32),
            pltpu.SemaphoreType.DMA((8,)),
        ],
    )
    kv, q_wire = lax.optimization_barrier((kv, q_wire))
    q_far = permute(q_wire, lambda i: i ^ top)
    r2 = permute(kv, second)
    q_far, r2 = lax.optimization_barrier((q_far, r2))
    r3 = permute(r1, second)
    held = [(kv, (0, 0)), (r1, (2, 4)), (r2, (4, 2)), (r3, (6, 6))]
    for bit in range(3, bits - 1):
        step = 1 << bit
        held = held + [
            (permute(piece, lambda i: i ^ step), (a ^ step, b ^ step)) for piece, (a, b) in held
        ]

    k_next = permute(k_wire, lambda i: i ^ 2)
    kv_here, i_own = call(
        stage_kernel,
        (shape((WIDTH, TOK), BF), shape((I_ROWS, IDX), BF)),
        "stage",
        0,
        kv,
        i_own,
        specs=[HBM] * 2,
        scratch=[pltpu.SemaphoreType.DMA((2,))],
    )
    kv_core = swap(kv_here)
    keys = [k_wire, swap(k_wire), k_next, swap(k_next)]

    def unpack(name, flops, *args):
        outs = [shape((ROWS, WIDTH), BF), shape((rows, TOK), F32)]
        if len(args) == 3:
            outs.append(shape((2 * I_ROWS, IDX), BF))
        return call(functools.partial(unpack_kernel, half_size), tuple(outs), name, flops, *args)

    q_far, *keys = lax.optimization_barrier((q_far, *keys))
    q_there, bias_there, i_pair = unpack("unpack_far", 3 * 1.15e9, q_far, q_far, i_own)
    q_here, bias_here = unpack("unpack_own", 0, q_wire, bias_own)

    def pair(item):
        piece, (a, b) = item
        return [item, (swap(piece), (1 ^ b, 1 ^ a))]

    def run(q, bias, groups, last, name, state=None):
        for k, group in enumerate(groups):
            mode = last if k == len(groups) - 1 else "state"
            state = attend(half_size, q, bias, group, state, mode, f"{name}_{k}")
        return state

    near = [[(kv_here, (0, 0)), (kv_core, (1, 1))]] + [pair(item) for item in held[1:3]]
    (own0, own1), (r1a, r1b), (r2a, r2b) = near
    far = attend(half_size, q_there, bias_there, [own0, r1a, r2a], None, "state", "far_early")
    i_pairs = [i_pair]
    for bit in range(2, bits - 1):
        step = 1 << bit
        i_pairs = i_pairs + [permute(x, lambda i: i ^ step) for x in i_pairs]
    far, r3 = lax.optimization_barrier((far, r3))
    held[3] = (r3, held[3][1])
    late = [pair(item) for item in held[3:]]
    rest = sum(late[1:], [])
    groups = [[own1, r1b, r2b, late[0][0]], [late[0][1]]]
    groups += [rest[at : at + 6] for at in range(0, len(rest), 6)]
    far = run(q_there, bias_there, groups[:-1], "state", "far_late", far)
    prepared = call(
        pairs_kernel,
        (shape((2 * I_W, IDX), BF), shape((2, IH, 16), F32)) * len(i_pairs),
        "index_pairs",
        6 * 1.15e9,
        *i_pairs,
    )
    *far, prepared = lax.optimization_barrier((*far, prepared))
    wire = attend(half_size, q_there, bias_there, groups[-1], far, "wire", "far_last")
    wire, lse_far = wire
    o_far = permute(wire, lambda i: i ^ top)

    parts = call(
        functools.partial(score_kernel, len(i_pairs)),
        tuple(shape((4, 4 * TOK), F32) for _ in i_pairs),
        "index_scores",
        2 * len(i_pairs) * 4 * IH * 4 * TOK * IDX,
        *prepared,
        *keys,
    )
    parts = [[(part, 0)] for part in parts]
    for bit in reversed(range(2, bits - 1)):
        step = 1 << bit
        count = len(parts) // 2
        parts = [
            parts[j] + [(permute(x, lambda i: i ^ step), mask ^ step) for x, mask in parts[j + count]]
            for j in range(count)
        ]
    late = [sum(near + late[:1], [])] + groups[2:]
    o_own, lse_own = run(q_here, bias_here, late, "own", "own_late")
    ranges, o_own = lax.optimization_barrier((parts[0], o_own))
    scores_own, scores_far = call(
        functools.partial(order_kernel, half_size, tuple(mask for _, mask in parts[0])),
        (shape((2, half_size * TOK), F32), shape((2, half_size * TOK + 3 * HEADS), BF)),
        "order_scores",
        0,
        *[x for x, _ in ranges],
        lse_far,
    )
    scores_far = permute(scores_far, lambda i: i ^ top)

    return call(
        functools.partial(finish_kernel, half_size),
        (shape((2, n * TOK), F32), shape((2, HEADS, KVR), BF)),
        "finish",
        ROWS * KVR * 4,
        o_own,
        lse_own,
        o_far,
        scores_own,
        scores_far,
    )


def solution(mesh):
    spec = P(("groups", "ctx"))
    return jax.shard_map(
        functools.partial(local, mesh.shape["ctx"]),
        mesh=mesh,
        in_specs=(spec,) * 8,
        out_specs=(spec, spec),
        check_vma=False,
    )
```

```python
import functools

import jax
import jax.numpy as jnp
from jax import lax
from jax.experimental import pallas as pl
from jax.experimental.pallas import tpu as pltpu
from jax.sharding import PartitionSpec as P

BLOCK = 64
LANES = 512
KVR = 512
ROPE = 64
HEADS = 128
IH = 32
IDX = 128
TOK = 512
NEG = -1e30
LOG2E = 1.4426950408889634
TO_LOG2 = 192.0 ** (-0.5) * LOG2E

WIDTH = KVR + ROPE
ROWS = 2 * HEADS
CHUNKS = TOK // 128

I_W = 2 * IH
I_ROWS = I_W + 16
K_ROWS = TOK + 16

Q_IDX = 2 * WIDTH
Q_BIAS = Q_IDX + I_ROWS

BF = jnp.bfloat16
F32 = jnp.float32
VMEM = pl.BlockSpec(memory_space=pltpu.VMEM)
HBM = pl.BlockSpec(memory_space=pltpu.HBM)


def nn(a, b):
    return lax.dot_general(a, b, (((1,), (0,)), ((), ())), preferred_element_type=F32)


def nt(a, b):
    return lax.dot_general(a, b, (((1,), (1,)), ((), ())), preferred_element_type=F32)


def iota(shape, dim):
    return lax.broadcasted_iota(jnp.int32, shape, dim)


def onehot(cond):
    return jnp.where(cond, 1.0, 0.0).astype(BF)


def eye(n):
    return onehot(iota((n, n), 0) == iota((n, n), 1))


def pack_kernel(
    half_size, q_in, iq_in, w_in, keys_in, scale_in, sel_in, want_in,
    wire_ref, own_ref, k_ref, i_ref, w_ref, scale_ref, sel_ref, want_ref, bias, sems,
):
    moves = [
        (sel_in, sel_ref),
        (want_in, want_ref),
        (w_in, w_ref),
        (scale_in, scale_ref),
        (q_in, wire_ref.at[0:Q_IDX]),
        (iq_in, wire_ref.at[Q_IDX : Q_IDX + I_W]),
        (keys_in, k_ref.at[0:TOK]),
        (iq_in, i_ref.at[0:I_W]),
    ]
    copies = [
        pltpu.make_async_copy(src, dst, sems.at[k]) for k, (src, dst) in enumerate(moves)
    ]
    for copy in copies:
        copy.start()
    wire_ref[Q_IDX + I_W : Q_BIAS, :] = jnp.zeros((16, IDX), BF)
    i_ref[I_W:I_ROWS, :] = jnp.zeros((16, IDX), BF)
    k_ref[TOK:K_ROWS, :] = jnp.zeros((16, IDX), BF)
    for copy in copies[:4]:
        copy.wait()
    wire_ref[Q_IDX + I_W : Q_IDX + I_W + 2, 0:IH] = w_ref[...]
    i_ref[I_W : I_W + 2, 0:IH] = w_ref[...]
    k_ref[TOK : TOK + CHUNKS, :] = scale_ref[...]
    me = lax.axis_index("ctx")
    half = me // half_size
    n = 2 * half_size
    slots = want_ref.shape[0]
    topk = sel_ref.shape[1]
    asked = nt(eye(n), want_ref[...].astype(F32).astype(BF))
    lane_block = (iota((n, LANES), 1) // BLOCK).astype(F32)
    spread = onehot(iota((BLOCK, LANES), 1) % BLOCK == iota((BLOCK, LANES), 0))
    line = iota((slots * n, topk), 0)
    slot_of_line = (line % n) * slots + line // n
    for t in range(2):
        sel = sel_ref[t : t + 1, :]
        inner = onehot(sel % BLOCK == iota((BLOCK, topk), 0))
        count = nt(onehot(sel // BLOCK == slot_of_line), inner)
        wide = nn(count.astype(BF), spread)
        total = jnp.zeros((n, LANES), F32)
        for b in range(slots):
            total = total + jnp.where(
                lane_block == asked[:, b : b + 1], wide[b * n : (b + 1) * n, :], 0.0
            )
        bias[t] = jnp.where(total > 0.5, 0.0, NEG)
    mine = pl.multiple_of(half * half_size, half_size)
    other = pl.multiple_of((1 - half) * half_size, half_size)
    rows = 2 * half_size
    for c in range(CHUNKS):
        lanes = slice(c * 128, (c + 1) * 128)
        own_ref[c * rows : (c + 1) * rows, :] = jnp.concatenate(
            [bias[t, pl.ds(mine, half_size), lanes] for t in range(2)], axis=0
        ).astype(BF)
        wire_ref[Q_BIAS + c * rows : Q_BIAS + (c + 1) * rows, :] = jnp.concatenate(
            [bias[t, pl.ds(other, half_size), lanes] for t in range(2)], axis=0
        ).astype(BF)
    for copy in copies[4:]:
        copy.wait()


def stage_kernel(kv_in, i_in, k_in, kv_ref, i_ref, k_ref, sems):
    copies = [
        pltpu.make_async_copy(kv_in, kv_ref, sems.at[0]),
        pltpu.make_async_copy(i_in, i_ref, sems.at[1]),
        pltpu.make_async_copy(k_in, k_ref, sems.at[2]),
    ]
    for copy in copies:
        copy.start()
    for copy in copies:
        copy.wait()


def unpack_kernel(half_size, *refs):
    if len(refs) == 6:
        wire_ref, bias_ref, own_ref, q_ref, out_ref, pair_ref = refs
        pair_ref[0:I_ROWS, :] = own_ref[...]
        pair_ref[I_ROWS : 2 * I_ROWS, :] = wire_ref[Q_IDX:Q_BIAS, :]
    else:
        wire_ref, bias_ref, q_ref, out_ref = refs
    for t in range(2):
        rows = nt(eye(HEADS), wire_ref[t * WIDTH : (t + 1) * WIDTH, :])
        q_ref[t * HEADS : (t + 1) * HEADS, :] = rows.astype(BF)
    rows = 2 * half_size
    base = bias_ref.shape[0] - CHUNKS * rows
    for c in range(CHUNKS):
        out_ref[:, c * 128 : (c + 1) * 128] = bias_ref[
            base + c * rows : base + (c + 1) * rows, :
        ].astype(F32)


def attend_kernel(half_size, masks, first, mode, queries, *refs):
    count = len(masks)
    refs = list(refs)
    q_ref, bias_ref = refs[:2]
    pieces = refs[2 : 2 + count]
    pos = 2 + count
    if not first:
        acc_in, m_in, l_in = refs[pos : pos + 3]
        pos += 3
    outs = refs[pos:-1]
    logits = refs[-1]

    me = lax.axis_index("ctx")
    core = me % 2
    span = slice(queries[0] * HEADS, (queries[-1] + 1) * HEADS)
    size = len(queries) * HEADS
    q = q_ref[span, :]
    m_prev = None if first else m_in[span, 0:1]
    m_new = m_prev
    for p in range(count):
        kv = pieces[p]
        src = lax.bitwise_xor(me, jnp.where(core == 0, masks[p][0], masks[p][1]))
        src = src % half_size
        s = nn(q, kv[0:WIDTH, :]) * TO_LOG2
        for k, t in enumerate(queries):
            part = s[k * HEADS : (k + 1) * HEADS, :] + bias_ref[pl.ds(t * half_size + src, 1), :]
            logits[k * HEADS : (k + 1) * HEADS, p * TOK : (p + 1) * TOK] = part
    top = jnp.max(logits[...], axis=1, keepdims=True)
    m_new = top if first else jnp.maximum(m_prev, top)

    total = None
    acc = None
    for p in range(count):
        e = jnp.exp2(logits[:, p * TOK : (p + 1) * TOK] - m_new)
        part = jnp.sum(e, axis=1, keepdims=True)
        total = part if total is None else total + part
        out = nt(e.astype(BF), pieces[p][0:KVR, :])
        acc = out if acc is None else acc + out
    if not first:
        alpha = jnp.exp2(m_prev - m_new)
        total = total + l_in[span, 0:1] * alpha
        acc = acc + acc_in[span, :] * alpha
    if mode == "state":
        acc_out, m_out, l_out = outs
        acc_out[...] = acc
        m_out[...] = jnp.broadcast_to(m_new, m_out.shape)
        l_out[...] = jnp.broadcast_to(total, l_out.shape)
        return
    norm = acc * (1.0 / total)
    lse = m_new + jnp.log(total) * LOG2E
    if mode == "own":
        o_out, lse_out = outs
        o_out[...] = norm
        lse_out[...] = jnp.broadcast_to(lse, lse_out.shape)
        return
    wire_out, lse_out = outs
    wire_out[...] = norm.astype(BF)
    diag = iota((HEADS, HEADS), 0) == iota((HEADS, HEADS), 1)
    for t in range(2):
        column = lse[t * HEADS : (t + 1) * HEADS, :]
        lse_out[t : t + 1, :] = jnp.sum(jnp.where(diag, column, 0.0), axis=0, keepdims=True)


def pairs_kernel(*refs):
    pairs, outs = refs[: len(refs) // 3], refs[len(refs) // 3 :]
    for j, pair in enumerate(pairs):
        q_ref, w_ref = outs[2 * j : 2 * j + 2]
        for k in range(2):
            at = k * I_ROWS
            q_ref[k * I_W : (k + 1) * I_W, :] = pair[at : at + I_W, :]
            w_ref[k] = nt(eye(IH), pair[at + I_W : at + I_ROWS, 0:IH])


def score_kernel(count, *refs):
    pairs, refs = refs[: 2 * count], refs[2 * count :]
    keys, outs = refs[:4], refs[4:]
    me = lax.axis_index("ctx")
    for j, out in enumerate(outs):
        both = pairs[2 * j][...]
        w_cols = [pairs[2 * j + 1][k] for k in range(2)]
        for p in range(4):
            raw = jnp.maximum(nt(both, keys[p][0:TOK, :]), 0.0)
            scales = keys[p][TOK:K_ROWS, :].astype(F32)
            scale = jnp.concatenate([scales[c : c + 1, :] for c in range(CHUNKS)], axis=1)
            at = pl.multiple_of(lax.bitwise_and(lax.bitwise_xor(me, p), 3) * TOK, TOK)
            for side in range(2):
                for t in range(2):
                    row = side * 2 + t
                    weighted = raw[row * IH : (row + 1) * IH, :] * w_cols[side][:, t : t + 1]
                    line = jnp.sum(weighted, axis=0, keepdims=True) * scale
                    out[row : row + 1, pl.ds(at, TOK)] = line


def order_kernel(half_size, masks, *refs):
    me = lax.axis_index("ctx")
    lse_ref, own_ref, far_ref = refs[-3:]
    span = 4 * TOK
    width = half_size * TOK
    hi = lse_ref[...].astype(BF)
    rest = lse_ref[...] - hi.astype(F32)
    mid = rest.astype(BF)
    parts = (hi, mid, (rest - mid.astype(F32)).astype(BF))
    for k, part in enumerate(parts):
        far_ref[:, width + k * HEADS : width + (k + 1) * HEADS] = part
    for ref, mask in zip(refs, masks):
        at = lax.bitwise_and(lax.bitwise_xor(me, mask), half_size - 1) // 4 * span
        at = pl.multiple_of(at, span)
        own_ref[:, pl.ds(at, span)] = ref[0:2, :]
        far_ref[:, pl.ds(at, span)] = ref[2:4, :].astype(BF)


def finish_kernel(half_size, o_ref, lse_ref, wire_ref, own_ref, far_ref, scores_ref, out_ref):
    half = lax.axis_index("ctx") // half_size
    width = half_size * TOK
    scores_ref[:, pl.ds(pl.multiple_of(half * width, width), width)] = own_ref[...]
    scores_ref[:, pl.ds(pl.multiple_of((1 - half) * width, width), width)] = far_ref[:, 0:width].astype(F32)
    stats = far_ref[:, width:].astype(F32)
    stats = stats[:, 0:HEADS] + stats[:, HEADS : 2 * HEADS] + stats[:, 2 * HEADS : 3 * HEADS]
    diag = iota((HEADS, HEADS), 0) == iota((HEADS, HEADS), 1)
    lse_r = jnp.concatenate(
        [
            jnp.sum(jnp.where(diag, stats[t : t + 1, :], 0.0), axis=1, keepdims=True)
            for t in range(2)
        ],
        axis=0,
    )
    lse_o = lse_ref[:, 0:1]
    top = jnp.maximum(lse_r, lse_o)
    e_r = jnp.exp2(lse_r - top)
    e_o = jnp.exp2(lse_o - top)
    inv = 1.0 / (e_r + e_o)
    out = o_ref[...] * (e_o * inv) + wire_ref[...].astype(F32) * (e_r * inv)
    for t in range(2):
        out_ref[t] = out[t * HEADS : (t + 1) * HEADS, :].astype(BF)


def call(kernel, out_shape, name, flops, *args, scratch=(), specs=None, limit=48 << 20):
    moved = sum(a.size * a.dtype.itemsize for a in args)
    return pl.pallas_call(
        kernel,
        out_shape=out_shape,
        in_specs=specs or [VMEM] * len(args),
        out_specs=jax.tree.map(lambda _: VMEM, out_shape),
        scratch_shapes=list(scratch),
        name=name,
        cost_estimate=pl.CostEstimate(flops=int(flops), bytes_accessed=moved, transcendentals=0),
        compiler_params=pltpu.CompilerParams(vmem_limit_bytes=limit),
    )(*args)


def shape(dims, dtype):
    return jax.ShapeDtypeStruct(dims, dtype)


def attend(half_size, q, bias, group, state, mode, name, queries=(0, 1)):
    masks = tuple(mask for _, mask in group)
    args = [q, bias] + [piece for piece, _ in group]
    size = len(queries) * HEADS
    state_shape = (shape((ROWS, KVR), F32), shape((ROWS, 128), F32), shape((ROWS, 128), F32))
    if state is not None:
        args += list(state)
    if mode == "state":
        outs = state_shape
    elif mode == "wire":
        outs = (shape((ROWS, KVR), BF), shape((2, HEADS), F32))
    else:
        outs = state_shape[:2]
    scratch = [pltpu.VMEM((size, TOK * len(group)), F32)]
    flops = 2 * size * TOK * len(group) * (2 * KVR + ROPE)
    return call(
        functools.partial(attend_kernel, half_size, masks, state is None, mode, queries),
        outs,
        name,
        flops,
        *args,
        scratch=scratch,
    )


def local(n, index_queries, index_weights, index_keys, key_scales, q_latent, latents, wanted, selected):
    half_size = n // 2
    bits = n.bit_length() - 1
    top = 1 << (bits - 1)

    def permute(x, move):
        return lax.ppermute(x, "ctx", [(i, move(i)) for i in range(n)])

    def swap(x):
        return permute(x, lambda i: i ^ 1)

    def first(i):
        return i ^ 2 if i % 2 == 0 else i ^ 4

    def second(i):
        return i ^ 4 if i % 2 == 0 else i ^ 2

    kv = latents.T
    r1 = permute(kv, first)

    rows = 2 * half_size
    q_wire, bias_own, k_wire, i_own = call(
        functools.partial(pack_kernel, half_size),
        (
            shape((Q_BIAS + CHUNKS * rows, 128), BF),
            shape((CHUNKS * rows, 128), BF),
            shape((K_ROWS, IDX), BF),
            shape((I_ROWS, IDX), BF),
        ),
        "pack",
        2 * 2 * n * 4 * 2048 * 64,
        jnp.swapaxes(q_latent, 1, 2).reshape(2 * WIDTH, HEADS),
        index_queries.reshape(2 * IH, IDX),
        index_weights,
        index_keys,
        key_scales.reshape(CHUNKS, 128),
        selected,
        wanted[0].T,
        specs=[HBM] * 7,
        limit=None,
        scratch=[
            pltpu.VMEM((2, IH), BF),
            pltpu.VMEM((CHUNKS, 128), BF),
            pltpu.VMEM(selected.shape, jnp.int32),
            pltpu.VMEM((wanted.shape[2], n), jnp.int32),
            pltpu.VMEM((2, n, LANES), F32),
            pltpu.SemaphoreType.DMA((8,)),
        ],
    )
    kv, q_wire = lax.optimization_barrier((kv, q_wire))
    q_far = permute(q_wire, lambda i: i ^ top)
    r2 = permute(kv, second)
    q_far, r2 = lax.optimization_barrier((q_far, r2))
    r3 = permute(r1, second)
    held = [(kv, (0, 0)), (r1, (2, 4)), (r2, (4, 2)), (r3, (6, 6))]
    for bit in range(3, bits - 1):
        step = 1 << bit
        held = held + [
            (permute(piece, lambda i: i ^ step), (a ^ step, b ^ step)) for piece, (a, b) in held
        ]

    k_next = permute(k_wire, lambda i: i ^ 2)
    kv_here, i_own, k_here = call(
        stage_kernel,
        (shape((WIDTH, TOK), BF), shape((I_ROWS, IDX), BF), shape((K_ROWS, IDX), BF)),
        "stage",
        0,
        kv,
        i_own,
        k_wire,
        specs=[HBM] * 3,
        scratch=[pltpu.SemaphoreType.DMA((3,))],
    )
    kv_core = swap(kv_here)
    keys = [k_here, swap(k_wire), k_next, swap(k_next)]

    def unpack(name, flops, *args):
        outs = [shape((ROWS, WIDTH), BF), shape((rows, TOK), F32)]
        if len(args) == 3:
            outs.append(shape((2 * I_ROWS, IDX), BF))
        return call(functools.partial(unpack_kernel, half_size), tuple(outs), name, flops, *args)

    q_far, *keys = lax.optimization_barrier((q_far, *keys))
    q_there, bias_there, i_pair = unpack("unpack_far", 3 * 1.15e9, q_far, q_far, i_own)
    q_here, bias_here = unpack("unpack_own", 0, q_wire, bias_own)

    def pair(item):
        piece, (a, b) = item
        return [item, (swap(piece), (1 ^ b, 1 ^ a))]

    def run(q, bias, groups, last, name, state=None):
        for k, group in enumerate(groups):
            mode = last if k == len(groups) - 1 else "state"
            state = attend(half_size, q, bias, group, state, mode, f"{name}_{k}")
        return state

    near = [[(kv_here, (0, 0)), (kv_core, (1, 1))]] + [pair(item) for item in held[1:3]]
    (own0, own1), (r1a, r1b), (r2a, r2b) = near
    far = attend(half_size, q_there, bias_there, [own0, own1, r1a, r2a], None, "state", "far_early")
    i_pairs = [i_pair]
    for bit in range(2, bits - 1):
        step = 1 << bit
        i_pairs = i_pairs + [permute(x, lambda i: i ^ step) for x in i_pairs]
    far, r3 = lax.optimization_barrier((far, r3))
    held[3] = (r3, held[3][1])
    late = [pair(item) for item in held[3:]]
    rest = sum(late[1:], [])
    groups = [[r1b, r2b, late[0][0]], [late[0][1]]]
    groups += [rest[at : at + 6] for at in range(0, len(rest), 6)]
    far = run(q_there, bias_there, groups[:-1], "state", "far_late", far)
    prepared = call(
        pairs_kernel,
        (shape((2 * I_W, IDX), BF), shape((2, IH, 16), F32)) * len(i_pairs),
        "index_pairs",
        6 * 1.15e9,
        *i_pairs,
    )
    *far, prepared = lax.optimization_barrier((*far, prepared))
    wire = attend(half_size, q_there, bias_there, groups[-1], far, "wire", "far_last")
    wire, lse_far = wire
    o_far = permute(wire, lambda i: i ^ top)

    parts = call(
        functools.partial(score_kernel, len(i_pairs)),
        tuple(shape((4, 4 * TOK), F32) for _ in i_pairs),
        "index_scores",
        2 * len(i_pairs) * 4 * IH * 4 * TOK * IDX,
        *prepared,
        *keys,
    )
    parts = [[(part, 0)] for part in parts]
    for bit in reversed(range(2, bits - 1)):
        step = 1 << bit
        count = len(parts) // 2
        parts = [
            parts[j] + [(permute(x, lambda i: i ^ step), mask ^ step) for x, mask in parts[j + count]]
            for j in range(count)
        ]
    pieces = sum(near + late[:1], [])
    own = attend(half_size, q_here, bias_here, pieces[:4], None, "state", "own_first")
    ranges, own = lax.optimization_barrier((parts[0], own))
    o_own, lse_own = run(
        q_here, bias_here, [pieces[4:]] + groups[2:], "own", "own_late", own
    )
    scores_own, scores_far = call(
        functools.partial(order_kernel, half_size, tuple(mask for _, mask in parts[0])),
        (shape((2, half_size * TOK), F32), shape((2, half_size * TOK + 3 * HEADS), BF)),
        "order_scores",
        0,
        *[x for x, _ in ranges],
        lse_far,
    )
    scores_far = permute(scores_far, lambda i: i ^ top)

    return call(
        functools.partial(finish_kernel, half_size),
        (shape((2, n * TOK), F32), shape((2, HEADS, KVR), BF)),
        "finish",
        ROWS * KVR * 4,
        o_own,
        lse_own,
        o_far,
        scores_own,
        scores_far,
    )


def solution(mesh):
    spec = P(("groups", "ctx"))
    return jax.shard_map(
        functools.partial(local, mesh.shape["ctx"]),
        mesh=mesh,
        in_specs=(spec,) * 8,
        out_specs=(spec, spec),
        check_vma=False,
    )
```

```python
import functools

import jax
import jax.numpy as jnp
from jax import lax
from jax.experimental import pallas as pl
from jax.experimental.pallas import tpu as pltpu
from jax.sharding import PartitionSpec as P

BLOCK = 64
LANES = 512
KVR = 512
ROPE = 64
HEADS = 128
IH = 32
IDX = 128
TOK = 512
NEG = -1e30
LOG2E = 1.4426950408889634
TO_LOG2 = 192.0 ** (-0.5) * LOG2E

WIDTH = KVR + ROPE
ROWS = 2 * HEADS
CHUNKS = TOK // 128

I_W = 2 * IH
I_ROWS = I_W + 16
K_ROWS = TOK + 16

Q_IDX = 2 * WIDTH
Q_BIAS = Q_IDX + I_ROWS

BF = jnp.bfloat16
F32 = jnp.float32
VMEM = pl.BlockSpec(memory_space=pltpu.VMEM)
HBM = pl.BlockSpec(memory_space=pltpu.HBM)


def nn(a, b):
    return lax.dot_general(a, b, (((1,), (0,)), ((), ())), preferred_element_type=F32)


def nt(a, b):
    return lax.dot_general(a, b, (((1,), (1,)), ((), ())), preferred_element_type=F32)


def iota(shape, dim):
    return lax.broadcasted_iota(jnp.int32, shape, dim)


def onehot(cond):
    return jnp.where(cond, 1.0, 0.0).astype(BF)


def eye(n):
    return onehot(iota((n, n), 0) == iota((n, n), 1))


def pack_kernel(
    half_size, q_in, iq_in, w_in, keys_in, scale_in, sel_in, want_in,
    wire_ref, own_ref, k_ref, i_ref, w_ref, scale_ref, sel_ref, want_ref, bias, sems,
):
    moves = [
        (sel_in, sel_ref),
        (want_in, want_ref),
        (w_in, w_ref),
        (scale_in, scale_ref),
        (q_in, wire_ref.at[0:Q_IDX]),
        (iq_in, wire_ref.at[Q_IDX : Q_IDX + I_W]),
        (keys_in, k_ref.at[0:TOK]),
        (iq_in, i_ref.at[0:I_W]),
    ]
    copies = [
        pltpu.make_async_copy(src, dst, sems.at[k]) for k, (src, dst) in enumerate(moves)
    ]
    for copy in copies:
        copy.start()
    wire_ref[Q_IDX + I_W : Q_BIAS, :] = jnp.zeros((16, IDX), BF)
    i_ref[I_W:I_ROWS, :] = jnp.zeros((16, IDX), BF)
    k_ref[TOK:K_ROWS, :] = jnp.zeros((16, IDX), BF)
    for copy in copies[:4]:
        copy.wait()
    wire_ref[Q_IDX + I_W : Q_IDX + I_W + 2, 0:IH] = w_ref[...]
    i_ref[I_W : I_W + 2, 0:IH] = w_ref[...]
    k_ref[TOK : TOK + CHUNKS, :] = scale_ref[...]
    me = lax.axis_index("ctx")
    half = me // half_size
    n = 2 * half_size
    slots = want_ref.shape[0]
    topk = sel_ref.shape[1]
    asked = nt(eye(n), want_ref[...].astype(F32).astype(BF))
    lane_block = (iota((n, LANES), 1) // BLOCK).astype(F32)
    spread = onehot(iota((BLOCK, LANES), 1) % BLOCK == iota((BLOCK, LANES), 0))
    line = iota((slots * n, topk), 0)
    slot_of_line = (line % n) * slots + line // n
    for t in range(2):
        sel = sel_ref[t : t + 1, :]
        inner = onehot(sel % BLOCK == iota((BLOCK, topk), 0))
        count = nt(onehot(sel // BLOCK == slot_of_line), inner)
        wide = nn(count.astype(BF), spread)
        total = jnp.zeros((n, LANES), F32)
        for b in range(slots):
            total = total + jnp.where(
                lane_block == asked[:, b : b + 1], wide[b * n : (b + 1) * n, :], 0.0
            )
        bias[t] = jnp.where(total > 0.5, 0.0, NEG)
    mine = pl.multiple_of(half * half_size, half_size)
    other = pl.multiple_of((1 - half) * half_size, half_size)
    rows = 2 * half_size
    for c in range(CHUNKS):
        lanes = slice(c * 128, (c + 1) * 128)
        own_ref[c * rows : (c + 1) * rows, :] = jnp.concatenate(
            [bias[t, pl.ds(mine, half_size), lanes] for t in range(2)], axis=0
        ).astype(BF)
        wire_ref[Q_BIAS + c * rows : Q_BIAS + (c + 1) * rows, :] = jnp.concatenate(
            [bias[t, pl.ds(other, half_size), lanes] for t in range(2)], axis=0
        ).astype(BF)
    for copy in copies[4:]:
        copy.wait()


def stage_kernel(kv_in, i_in, k_in, kv_ref, i_ref, k_ref, sems):
    copies = [
        pltpu.make_async_copy(kv_in, kv_ref, sems.at[0]),
        pltpu.make_async_copy(i_in, i_ref, sems.at[1]),
        pltpu.make_async_copy(k_in, k_ref, sems.at[2]),
    ]
    for copy in copies:
        copy.start()
    for copy in copies:
        copy.wait()


def unpack_kernel(half_size, *refs):
    if len(refs) == 6:
        wire_ref, bias_ref, own_ref, q_ref, out_ref, pair_ref = refs
        pair_ref[0:I_ROWS, :] = own_ref[...]
        pair_ref[I_ROWS : 2 * I_ROWS, :] = wire_ref[Q_IDX:Q_BIAS, :]
    else:
        wire_ref, bias_ref, q_ref, out_ref = refs
    for t in range(2):
        rows = nt(eye(HEADS), wire_ref[t * WIDTH : (t + 1) * WIDTH, :])
        q_ref[t * HEADS : (t + 1) * HEADS, :] = rows.astype(BF)
    rows = 2 * half_size
    base = bias_ref.shape[0] - CHUNKS * rows
    for c in range(CHUNKS):
        out_ref[:, c * 128 : (c + 1) * 128] = bias_ref[
            base + c * rows : base + (c + 1) * rows, :
        ].astype(F32)


def attend_kernel(half_size, masks, first, mode, queries, *refs):
    count = len(masks)
    refs = list(refs)
    q_ref, bias_ref = refs[:2]
    pieces = refs[2 : 2 + count]
    pos = 2 + count
    if not first:
        acc_in, m_in, l_in = refs[pos : pos + 3]
        pos += 3
    outs = refs[pos:-1]
    logits = refs[-1]

    me = lax.axis_index("ctx")
    core = me % 2
    span = slice(queries[0] * HEADS, (queries[-1] + 1) * HEADS)
    size = len(queries) * HEADS
    q = q_ref[span, :]
    m_prev = None if first else m_in[span, 0:1]
    m_new = m_prev
    for p in range(count):
        kv = pieces[p]
        src = lax.bitwise_xor(me, jnp.where(core == 0, masks[p][0], masks[p][1]))
        src = src % half_size
        s = nn(q, kv[0:WIDTH, :]) * TO_LOG2
        for k, t in enumerate(queries):
            part = s[k * HEADS : (k + 1) * HEADS, :] + bias_ref[pl.ds(t * half_size + src, 1), :]
            logits[k * HEADS : (k + 1) * HEADS, p * TOK : (p + 1) * TOK] = part
    top = jnp.max(logits[...], axis=1, keepdims=True)
    m_new = top if first else jnp.maximum(m_prev, top)

    total = None
    acc = None
    for p in range(count):
        e = jnp.exp2(logits[:, p * TOK : (p + 1) * TOK] - m_new)
        part = jnp.sum(e, axis=1, keepdims=True)
        total = part if total is None else total + part
        out = nt(e.astype(BF), pieces[p][0:KVR, :])
        acc = out if acc is None else acc + out
    if not first:
        alpha = jnp.exp2(m_prev - m_new)
        total = total + l_in[span, 0:1] * alpha
        acc = acc + acc_in[span, :] * alpha
    if mode == "state":
        acc_out, m_out, l_out = outs
        acc_out[...] = acc
        m_out[...] = jnp.broadcast_to(m_new, m_out.shape)
        l_out[...] = jnp.broadcast_to(total, l_out.shape)
        return
    norm = acc * (1.0 / total)
    lse = m_new + jnp.log(total) * LOG2E
    if mode == "own":
        o_out, lse_out = outs
        o_out[...] = norm
        lse_out[...] = jnp.broadcast_to(lse, lse_out.shape)
        return
    wire_out, lse_out = outs
    wire_out[...] = norm.astype(BF)
    diag = iota((HEADS, HEADS), 0) == iota((HEADS, HEADS), 1)
    for t in range(2):
        column = lse[t * HEADS : (t + 1) * HEADS, :]
        lse_out[t : t + 1, :] = jnp.sum(jnp.where(diag, column, 0.0), axis=0, keepdims=True)


def pairs_kernel(*refs):
    pairs, outs = refs[: len(refs) // 3], refs[len(refs) // 3 :]
    for j, pair in enumerate(pairs):
        q_ref, w_ref = outs[2 * j : 2 * j + 2]
        for k in range(2):
            at = k * I_ROWS
            q_ref[k * I_W : (k + 1) * I_W, :] = pair[at : at + I_W, :]
            w_ref[k] = nt(eye(IH), pair[at + I_W : at + I_ROWS, 0:IH])


def score_kernel(count, *refs):
    pairs, refs = refs[: 2 * count], refs[2 * count :]
    keys, outs = refs[:4], refs[4:]
    me = lax.axis_index("ctx")
    for j, out in enumerate(outs):
        both = pairs[2 * j][...]
        w_cols = [pairs[2 * j + 1][k] for k in range(2)]
        for p in range(4):
            raw = jnp.maximum(nt(both, keys[p][0:TOK, :]), 0.0)
            scales = keys[p][TOK:K_ROWS, :].astype(F32)
            scale = jnp.concatenate([scales[c : c + 1, :] for c in range(CHUNKS)], axis=1)
            at = pl.multiple_of(lax.bitwise_and(lax.bitwise_xor(me, p), 3) * TOK, TOK)
            for side in range(2):
                for t in range(2):
                    row = side * 2 + t
                    weighted = raw[row * IH : (row + 1) * IH, :] * w_cols[side][:, t : t + 1]
                    line = jnp.sum(weighted, axis=0, keepdims=True) * scale
                    out[row : row + 1, pl.ds(at, TOK)] = line


def order_kernel(half_size, masks, *refs):
    me = lax.axis_index("ctx")
    lse_ref, own_ref, far_ref = refs[-3:]
    span = 4 * TOK
    width = half_size * TOK
    hi = lse_ref[...].astype(BF)
    rest = lse_ref[...] - hi.astype(F32)
    mid = rest.astype(BF)
    parts = (hi, mid, (rest - mid.astype(F32)).astype(BF))
    for k, part in enumerate(parts):
        far_ref[:, width + k * HEADS : width + (k + 1) * HEADS] = part
    for ref, mask in zip(refs, masks):
        at = lax.bitwise_and(lax.bitwise_xor(me, mask), half_size - 1) // 4 * span
        at = pl.multiple_of(at, span)
        own_ref[:, pl.ds(at, span)] = ref[0:2, :]
        far_ref[:, pl.ds(at, span)] = ref[2:4, :].astype(BF)


def finish_kernel(half_size, o_ref, lse_ref, wire_ref, own_ref, far_ref, scores_ref, out_ref):
    half = lax.axis_index("ctx") // half_size
    width = half_size * TOK
    scores_ref[:, pl.ds(pl.multiple_of(half * width, width), width)] = own_ref[...]
    scores_ref[:, pl.ds(pl.multiple_of((1 - half) * width, width), width)] = far_ref[:, 0:width].astype(F32)
    stats = far_ref[:, width:].astype(F32)
    stats = stats[:, 0:HEADS] + stats[:, HEADS : 2 * HEADS] + stats[:, 2 * HEADS : 3 * HEADS]
    diag = iota((HEADS, HEADS), 0) == iota((HEADS, HEADS), 1)
    lse_r = jnp.concatenate(
        [
            jnp.sum(jnp.where(diag, stats[t : t + 1, :], 0.0), axis=1, keepdims=True)
            for t in range(2)
        ],
        axis=0,
    )
    lse_o = lse_ref[:, 0:1]
    top = jnp.maximum(lse_r, lse_o)
    e_r = jnp.exp2(lse_r - top)
    e_o = jnp.exp2(lse_o - top)
    inv = 1.0 / (e_r + e_o)
    out = o_ref[...] * (e_o * inv) + wire_ref[...].astype(F32) * (e_r * inv)
    for t in range(2):
        out_ref[t] = out[t * HEADS : (t + 1) * HEADS, :].astype(BF)


def call(kernel, out_shape, name, flops, *args, scratch=(), specs=None, limit=48 << 20):
    moved = sum(a.size * a.dtype.itemsize for a in args)
    return pl.pallas_call(
        kernel,
        out_shape=out_shape,
        in_specs=specs or [VMEM] * len(args),
        out_specs=jax.tree.map(lambda _: VMEM, out_shape),
        scratch_shapes=list(scratch),
        name=name,
        cost_estimate=pl.CostEstimate(flops=int(flops), bytes_accessed=moved, transcendentals=0),
        compiler_params=pltpu.CompilerParams(vmem_limit_bytes=limit),
    )(*args)


def shape(dims, dtype):
    return jax.ShapeDtypeStruct(dims, dtype)


FACTOR = {"far_last": 2, "far_late_0": 0.3}


def attend(half_size, q, bias, group, state, mode, name, queries=(0, 1)):
    masks = tuple(mask for _, mask in group)
    args = [q, bias] + [piece for piece, _ in group]
    size = len(queries) * HEADS
    state_shape = (shape((ROWS, KVR), F32), shape((ROWS, 128), F32), shape((ROWS, 128), F32))
    if state is not None:
        args += list(state)
    if mode == "state":
        outs = state_shape
    elif mode == "wire":
        outs = (shape((ROWS, KVR), BF), shape((2, HEADS), F32))
    else:
        outs = state_shape[:2]
    scratch = [pltpu.VMEM((size, TOK * len(group)), F32)]
    flops = 2 * size * TOK * len(group) * (2 * KVR + ROPE) * FACTOR.get(name, 1)
    return call(
        functools.partial(attend_kernel, half_size, masks, state is None, mode, queries),
        outs,
        name,
        flops,
        *args,
        scratch=scratch,
    )


def local(n, index_queries, index_weights, index_keys, key_scales, q_latent, latents, wanted, selected):
    half_size = n // 2
    bits = n.bit_length() - 1
    top = 1 << (bits - 1)

    def permute(x, move):
        return lax.ppermute(x, "ctx", [(i, move(i)) for i in range(n)])

    def swap(x):
        return permute(x, lambda i: i ^ 1)

    def first(i):
        return i ^ 2 if i % 2 == 0 else i ^ 4

    def second(i):
        return i ^ 4 if i % 2 == 0 else i ^ 2

    kv = latents.T
    r1 = permute(kv, first)

    rows = 2 * half_size
    q_wire, bias_own, k_wire, i_own = call(
        functools.partial(pack_kernel, half_size),
        (
            shape((Q_BIAS + CHUNKS * rows, 128), BF),
            shape((CHUNKS * rows, 128), BF),
            shape((K_ROWS, IDX), BF),
            shape((I_ROWS, IDX), BF),
        ),
        "pack",
        0.1 * 1.15e9,
        jnp.swapaxes(q_latent, 1, 2).reshape(2 * WIDTH, HEADS),
        index_queries.reshape(2 * IH, IDX),
        index_weights,
        index_keys,
        key_scales.reshape(CHUNKS, 128),
        selected,
        wanted[0].T,
        specs=[HBM] * 7,
        limit=None,
        scratch=[
            pltpu.VMEM((2, IH), BF),
            pltpu.VMEM((CHUNKS, 128), BF),
            pltpu.VMEM(selected.shape, jnp.int32),
            pltpu.VMEM((wanted.shape[2], n), jnp.int32),
            pltpu.VMEM((2, n, LANES), F32),
            pltpu.SemaphoreType.DMA((8,)),
        ],
    )
    kv, q_wire = lax.optimization_barrier((kv, q_wire))
    q_far = permute(q_wire, lambda i: i ^ top)
    r2 = permute(kv, second)
    q_far, r2 = lax.optimization_barrier((q_far, r2))
    r3 = permute(r1, second)
    held = [(kv, (0, 0)), (r1, (2, 4)), (r2, (4, 2)), (r3, (6, 6))]
    for bit in range(3, bits - 1):
        step = 1 << bit
        held = held + [
            (permute(piece, lambda i: i ^ step), (a ^ step, b ^ step)) for piece, (a, b) in held
        ]

    k_next = permute(k_wire, lambda i: i ^ 2)
    kv_here, i_own, k_here = call(
        stage_kernel,
        (shape((WIDTH, TOK), BF), shape((I_ROWS, IDX), BF), shape((K_ROWS, IDX), BF)),
        "stage",
        0,
        kv,
        i_own,
        k_wire,
        specs=[HBM] * 3,
        scratch=[pltpu.SemaphoreType.DMA((3,))],
    )
    kv_core = swap(kv_here)
    keys = [k_here, swap(k_wire), k_next, swap(k_next)]

    def unpack(name, flops, *args):
        outs = [shape((ROWS, WIDTH), BF), shape((rows, TOK), F32)]
        if len(args) == 3:
            outs.append(shape((2 * I_ROWS, IDX), BF))
        return call(functools.partial(unpack_kernel, half_size), tuple(outs), name, flops, *args)

    q_far, r1, *keys = lax.optimization_barrier((q_far, r1, *keys))
    held[1] = (r1, held[1][1])
    q_there, bias_there, i_pair = unpack("unpack_far", 3 * 1.15e9, q_far, q_far, i_own)
    q_here, bias_here = unpack("unpack_own", 0, q_wire, bias_own)

    def pair(item):
        piece, (a, b) = item
        return [item, (swap(piece), (1 ^ b, 1 ^ a))]

    def run(q, bias, groups, last, name, state=None):
        for k, group in enumerate(groups):
            mode = last if k == len(groups) - 1 else "state"
            state = attend(half_size, q, bias, group, state, mode, f"{name}_{k}")
        return state

    near = [[(kv_here, (0, 0)), (kv_core, (1, 1))]] + [pair(item) for item in held[1:3]]
    (own0, own1), (r1a, r1b), (r2a, r2b) = near
    far = attend(half_size, q_there, bias_there, [own0, own1, r1a, r2a], None, "state", "far_early")
    i_pairs = [i_pair]
    for bit in range(2, bits - 1):
        step = 1 << bit
        i_pairs = i_pairs + [permute(x, lambda i: i ^ step) for x in i_pairs]
    far, r3 = lax.optimization_barrier((far, r3))
    held[3] = (r3, held[3][1])
    late = [pair(item) for item in held[3:]]
    rest = sum(late[1:], [])
    groups = [[r1b, r2b, late[0][0]], [late[0][1]]]
    groups += [rest[at : at + 6] for at in range(0, len(rest), 6)]
    far = run(q_there, bias_there, groups[:-1], "state", "far_late", far)
    prepared = call(
        pairs_kernel,
        (shape((2 * I_W, IDX), BF), shape((2, IH, 16), F32)) * len(i_pairs),
        "index_pairs",
        5 * 1.15e9,
        *i_pairs,
    )
    *far, prepared = lax.optimization_barrier((*far, prepared))
    wire = attend(half_size, q_there, bias_there, groups[-1], far, "wire", "far_last")
    wire, lse_far = wire
    o_far = permute(wire, lambda i: i ^ top)

    parts = call(
        functools.partial(score_kernel, len(i_pairs)),
        tuple(shape((4, 4 * TOK), F32) for _ in i_pairs),
        "index_scores",
        2 * len(i_pairs) * 4 * IH * 4 * TOK * IDX,
        *prepared,
        *keys,
    )
    parts = [[(part, 0)] for part in parts]
    for bit in reversed(range(2, bits - 1)):
        step = 1 << bit
        count = len(parts) // 2
        parts = [
            parts[j] + [(permute(x, lambda i: i ^ step), mask ^ step) for x, mask in parts[j + count]]
            for j in range(count)
        ]
    pieces = sum(near + late[:1], [])
    own = attend(half_size, q_here, bias_here, pieces[:4], None, "state", "own_first")
    ranges, own = lax.optimization_barrier((parts[0], own))
    o_own, lse_own = run(
        q_here, bias_here, [pieces[4:]] + groups[2:], "own", "own_late", own
    )
    scores_own, scores_far = call(
        functools.partial(order_kernel, half_size, tuple(mask for _, mask in parts[0])),
        (shape((2, half_size * TOK), F32), shape((2, half_size * TOK + 3 * HEADS), BF)),
        "order_scores",
        0,
        *[x for x, _ in ranges],
        lse_far,
    )
    scores_far = permute(scores_far, lambda i: i ^ top)

    return call(
        functools.partial(finish_kernel, half_size),
        (shape((2, n * TOK), F32), shape((2, HEADS, KVR), BF)),
        "finish",
        5 * 1.15e9,
        o_own,
        lse_own,
        o_far,
        scores_own,
        scores_far,
    )


def solution(mesh):
    spec = P(("groups", "ctx"))
    return jax.shard_map(
        functools.partial(local, mesh.shape["ctx"]),
        mesh=mesh,
        in_specs=(spec,) * 8,
        out_specs=(spec, spec),
        check_vma=False,
    )
```

```python
import functools

import jax
import jax.numpy as jnp
from jax import lax
from jax.experimental import pallas as pl
from jax.experimental.pallas import tpu as pltpu
from jax.sharding import PartitionSpec as P

BLOCK = 64
LANES = 512
KVR = 512
ROPE = 64
HEADS = 128
IH = 32
IDX = 128
TOK = 512
NEG = -1e30
LOG2E = 1.4426950408889634
TO_LOG2 = 192.0 ** (-0.5) * LOG2E

WIDTH = KVR + ROPE
ROWS = 2 * HEADS
CHUNKS = TOK // 128

I_W = 2 * IH
I_ROWS = I_W + 16
K_ROWS = TOK + 16

Q_IDX = 2 * WIDTH
Q_BIAS = Q_IDX + I_ROWS

BF = jnp.bfloat16
F32 = jnp.float32
VMEM = pl.BlockSpec(memory_space=pltpu.VMEM)
HBM = pl.BlockSpec(memory_space=pltpu.HBM)


def nn(a, b):
    return lax.dot_general(a, b, (((1,), (0,)), ((), ())), preferred_element_type=F32)


def nt(a, b):
    return lax.dot_general(a, b, (((1,), (1,)), ((), ())), preferred_element_type=F32)


def iota(shape, dim):
    return lax.broadcasted_iota(jnp.int32, shape, dim)


def onehot(cond):
    return jnp.where(cond, 1.0, 0.0).astype(BF)


def eye(n):
    return onehot(iota((n, n), 0) == iota((n, n), 1))


def pack_kernel(
    half_size, q_in, iq_in, w_in, keys_in, scale_in, sel_in, want_in,
    wire_ref, own_ref, k_ref, i_ref, w_ref, scale_ref, sel_ref, want_ref, bias, sems,
):
    moves = [
        (sel_in, sel_ref),
        (want_in, want_ref),
        (w_in, w_ref),
        (scale_in, scale_ref),
        (q_in, wire_ref.at[0:Q_IDX]),
        (iq_in, wire_ref.at[Q_IDX : Q_IDX + I_W]),
        (keys_in, k_ref.at[0:TOK]),
        (iq_in, i_ref.at[0:I_W]),
    ]
    copies = [
        pltpu.make_async_copy(src, dst, sems.at[k]) for k, (src, dst) in enumerate(moves)
    ]
    for copy in copies:
        copy.start()
    wire_ref[Q_IDX + I_W : Q_BIAS, :] = jnp.zeros((16, IDX), BF)
    i_ref[I_W:I_ROWS, :] = jnp.zeros((16, IDX), BF)
    k_ref[TOK:K_ROWS, :] = jnp.zeros((16, IDX), BF)
    for copy in copies[:4]:
        copy.wait()
    wire_ref[Q_IDX + I_W : Q_IDX + I_W + 2, 0:IH] = w_ref[...]
    i_ref[I_W : I_W + 2, 0:IH] = w_ref[...]
    k_ref[TOK : TOK + CHUNKS, :] = scale_ref[...]
    me = lax.axis_index("ctx")
    half = me // half_size
    n = 2 * half_size
    slots = want_ref.shape[0]
    topk = sel_ref.shape[1]
    asked = nt(eye(n), want_ref[...].astype(F32).astype(BF))
    lane_block = (iota((n, LANES), 1) // BLOCK).astype(F32)
    spread = onehot(iota((BLOCK, LANES), 1) % BLOCK == iota((BLOCK, LANES), 0))
    line = iota((slots * n, topk), 0)
    slot_of_line = (line % n) * slots + line // n
    for t in range(2):
        sel = sel_ref[t : t + 1, :]
        inner = onehot(sel % BLOCK == iota((BLOCK, topk), 0))
        count = nt(onehot(sel // BLOCK == slot_of_line), inner)
        wide = nn(count.astype(BF), spread)
        total = jnp.zeros((n, LANES), F32)
        for b in range(slots):
            total = total + jnp.where(
                lane_block == asked[:, b : b + 1], wide[b * n : (b + 1) * n, :], 0.0
            )
        bias[t] = jnp.where(total > 0.5, 0.0, NEG)
    mine = pl.multiple_of(half * half_size, half_size)
    other = pl.multiple_of((1 - half) * half_size, half_size)
    rows = 2 * half_size
    for c in range(CHUNKS):
        lanes = slice(c * 128, (c + 1) * 128)
        own_ref[c * rows : (c + 1) * rows, :] = jnp.concatenate(
            [bias[t, pl.ds(mine, half_size), lanes] for t in range(2)], axis=0
        ).astype(BF)
        wire_ref[Q_BIAS + c * rows : Q_BIAS + (c + 1) * rows, :] = jnp.concatenate(
            [bias[t, pl.ds(other, half_size), lanes] for t in range(2)], axis=0
        ).astype(BF)
    for copy in copies[4:]:
        copy.wait()


def stage_kernel(kv_in, i_in, k_in, kv_ref, i_ref, k_ref, sems):
    copies = [
        pltpu.make_async_copy(kv_in, kv_ref, sems.at[0]),
        pltpu.make_async_copy(i_in, i_ref, sems.at[1]),
        pltpu.make_async_copy(k_in, k_ref, sems.at[2]),
    ]
    for copy in copies:
        copy.start()
    for copy in copies:
        copy.wait()


def unpack_kernel(half_size, *refs):
    if len(refs) == 6:
        wire_ref, bias_ref, own_ref, q_ref, out_ref, pair_ref = refs
        pair_ref[0:I_ROWS, :] = own_ref[...]
        pair_ref[I_ROWS : 2 * I_ROWS, :] = wire_ref[Q_IDX:Q_BIAS, :]
    else:
        wire_ref, bias_ref, q_ref, out_ref = refs
    for t in range(2):
        rows = nt(eye(HEADS), wire_ref[t * WIDTH : (t + 1) * WIDTH, :])
        q_ref[t * HEADS : (t + 1) * HEADS, :] = rows.astype(BF)
    rows = 2 * half_size
    base = bias_ref.shape[0] - CHUNKS * rows
    for c in range(CHUNKS):
        out_ref[:, c * 128 : (c + 1) * 128] = bias_ref[
            base + c * rows : base + (c + 1) * rows, :
        ].astype(F32)


def attend_kernel(half_size, masks, first, mode, queries, *refs):
    count = len(masks)
    refs = list(refs)
    q_ref, bias_ref = refs[:2]
    pieces = refs[2 : 2 + count]
    pos = 2 + count
    if not first:
        acc_in, m_in, l_in = refs[pos : pos + 3]
        pos += 3
    outs = refs[pos:-1]
    logits = refs[-1]

    me = lax.axis_index("ctx")
    core = me % 2
    span = slice(queries[0] * HEADS, (queries[-1] + 1) * HEADS)
    size = len(queries) * HEADS
    q = q_ref[span, :]
    m_prev = None if first else m_in[span, 0:1]
    m_new = m_prev
    for p in range(count):
        kv = pieces[p]
        src = lax.bitwise_xor(me, jnp.where(core == 0, masks[p][0], masks[p][1]))
        src = src % half_size
        s = nn(q, kv[0:WIDTH, :]) * TO_LOG2
        for k, t in enumerate(queries):
            part = s[k * HEADS : (k + 1) * HEADS, :] + bias_ref[pl.ds(t * half_size + src, 1), :]
            logits[k * HEADS : (k + 1) * HEADS, p * TOK : (p + 1) * TOK] = part
    top = jnp.max(logits[...], axis=1, keepdims=True)
    m_new = top if first else jnp.maximum(m_prev, top)

    total = None
    acc = None
    for p in range(count):
        e = jnp.exp2(logits[:, p * TOK : (p + 1) * TOK] - m_new)
        part = jnp.sum(e, axis=1, keepdims=True)
        total = part if total is None else total + part
        out = nt(e.astype(BF), pieces[p][0:KVR, :])
        acc = out if acc is None else acc + out
    if not first:
        alpha = jnp.exp2(m_prev - m_new)
        total = total + l_in[span, 0:1] * alpha
        acc = acc + acc_in[span, :] * alpha
    if mode == "state":
        acc_out, m_out, l_out = outs
        acc_out[...] = acc
        m_out[...] = jnp.broadcast_to(m_new, m_out.shape)
        l_out[...] = jnp.broadcast_to(total, l_out.shape)
        return
    norm = acc * (1.0 / total)
    lse = m_new + jnp.log(total) * LOG2E
    if mode == "own":
        o_out, lse_out = outs
        o_out[...] = norm
        lse_out[...] = jnp.broadcast_to(lse, lse_out.shape)
        return
    wire_out, lse_out = outs
    wire_out[...] = norm.astype(BF)
    diag = iota((HEADS, HEADS), 0) == iota((HEADS, HEADS), 1)
    for t in range(2):
        column = lse[t * HEADS : (t + 1) * HEADS, :]
        lse_out[t : t + 1, :] = jnp.sum(jnp.where(diag, column, 0.0), axis=0, keepdims=True)


def pairs_kernel(*refs):
    pairs, outs = refs[: len(refs) // 3], refs[len(refs) // 3 :]
    for j, pair in enumerate(pairs):
        q_ref, w_ref = outs[2 * j : 2 * j + 2]
        for k in range(2):
            at = k * I_ROWS
            q_ref[k * I_W : (k + 1) * I_W, :] = pair[at : at + I_W, :]
            w_ref[k] = nt(eye(IH), pair[at + I_W : at + I_ROWS, 0:IH])


def score_kernel(count, *refs):
    pairs, refs = refs[: 2 * count], refs[2 * count :]
    keys, outs = refs[:4], refs[4:]
    me = lax.axis_index("ctx")
    for j, out in enumerate(outs):
        both = pairs[2 * j][...]
        w_cols = [pairs[2 * j + 1][k] for k in range(2)]
        for p in range(4):
            raw = jnp.maximum(nt(both, keys[p][0:TOK, :]), 0.0)
            scales = keys[p][TOK:K_ROWS, :].astype(F32)
            scale = jnp.concatenate([scales[c : c + 1, :] for c in range(CHUNKS)], axis=1)
            at = pl.multiple_of(lax.bitwise_and(lax.bitwise_xor(me, p), 3) * TOK, TOK)
            lines = []
            for row in range(4):
                weighted = raw[row * IH : (row + 1) * IH, :] * w_cols[row // 2][:, row % 2 : row % 2 + 1]
                lines.append(jnp.sum(weighted, axis=0, keepdims=True) * scale)
            out[:, pl.ds(at, TOK)] = jnp.concatenate(lines, axis=0).astype(out.dtype)


def order_kernel(half_size, masks, *refs):
    me = lax.axis_index("ctx")
    lse_ref, own_ref, far_ref = refs[-3:]
    span = 4 * TOK
    width = half_size * TOK
    hi = lse_ref[...].astype(BF)
    rest = lse_ref[...] - hi.astype(F32)
    mid = rest.astype(BF)
    parts = (hi, mid, (rest - mid.astype(F32)).astype(BF))
    for k, part in enumerate(parts):
        far_ref[:, width + k * HEADS : width + (k + 1) * HEADS] = part
    for ref, mask in zip(refs, masks):
        at = lax.bitwise_and(lax.bitwise_xor(me, mask), half_size - 1) // 4 * span
        at = pl.multiple_of(at, span)
        lines = ref[...].astype(F32)
        own_ref[:, pl.ds(at, span)] = lines[0:2, :]
        far_ref[:, pl.ds(at, span)] = lines[2:4, :].astype(BF)


def finish_kernel(half_size, o_ref, lse_ref, wire_ref, own_ref, far_ref, scores_ref, out_ref):
    half = lax.axis_index("ctx") // half_size
    width = half_size * TOK
    scores_ref[:, pl.ds(pl.multiple_of(half * width, width), width)] = own_ref[...]
    scores_ref[:, pl.ds(pl.multiple_of((1 - half) * width, width), width)] = far_ref[:, 0:width].astype(F32)
    stats = far_ref[:, width:].astype(F32)
    stats = stats[:, 0:HEADS] + stats[:, HEADS : 2 * HEADS] + stats[:, 2 * HEADS : 3 * HEADS]
    diag = iota((HEADS, HEADS), 0) == iota((HEADS, HEADS), 1)
    lse_r = jnp.concatenate(
        [
            jnp.sum(jnp.where(diag, stats[t : t + 1, :], 0.0), axis=1, keepdims=True)
            for t in range(2)
        ],
        axis=0,
    )
    lse_o = lse_ref[:, 0:1]
    top = jnp.maximum(lse_r, lse_o)
    e_r = jnp.exp2(lse_r - top)
    e_o = jnp.exp2(lse_o - top)
    inv = 1.0 / (e_r + e_o)
    out = o_ref[...] * (e_o * inv) + wire_ref[...].astype(F32) * (e_r * inv)
    for t in range(2):
        out_ref[t] = out[t * HEADS : (t + 1) * HEADS, :].astype(BF)


def call(kernel, out_shape, name, flops, *args, scratch=(), specs=None, limit=48 << 20):
    moved = sum(a.size * a.dtype.itemsize for a in args)
    return pl.pallas_call(
        kernel,
        out_shape=out_shape,
        in_specs=specs or [VMEM] * len(args),
        out_specs=jax.tree.map(lambda _: VMEM, out_shape),
        scratch_shapes=list(scratch),
        name=name,
        cost_estimate=pl.CostEstimate(flops=int(flops), bytes_accessed=moved, transcendentals=0),
        compiler_params=pltpu.CompilerParams(vmem_limit_bytes=limit),
    )(*args)


def shape(dims, dtype):
    return jax.ShapeDtypeStruct(dims, dtype)


def attend(half_size, q, bias, group, state, mode, name, queries=(0, 1)):
    masks = tuple(mask for _, mask in group)
    args = [q, bias] + [piece for piece, _ in group]
    size = len(queries) * HEADS
    state_shape = (shape((ROWS, KVR), F32), shape((ROWS, 128), F32), shape((ROWS, 128), F32))
    if state is not None:
        args += list(state)
    if mode == "state":
        outs = state_shape
    elif mode == "wire":
        outs = (shape((ROWS, KVR), BF), shape((2, HEADS), F32))
    else:
        outs = state_shape[:2]
    scratch = [pltpu.VMEM((size, TOK * len(group)), F32)]
    flops = 2 * size * TOK * len(group) * (2 * KVR + ROPE)
    return call(
        functools.partial(attend_kernel, half_size, masks, state is None, mode, queries),
        outs,
        name,
        flops,
        *args,
        scratch=scratch,
    )


def local(n, index_queries, index_weights, index_keys, key_scales, q_latent, latents, wanted, selected):
    half_size = n // 2
    bits = n.bit_length() - 1
    top = 1 << (bits - 1)

    def permute(x, move):
        return lax.ppermute(x, "ctx", [(i, move(i)) for i in range(n)])

    def swap(x):
        return permute(x, lambda i: i ^ 1)

    def first(i):
        return i ^ 2 if i % 2 == 0 else i ^ 4

    def second(i):
        return i ^ 4 if i % 2 == 0 else i ^ 2

    kv = latents.T
    r1 = permute(kv, first)

    rows = 2 * half_size
    q_wire, bias_own, k_wire, i_own = call(
        functools.partial(pack_kernel, half_size),
        (
            shape((Q_BIAS + CHUNKS * rows, 128), BF),
            shape((CHUNKS * rows, 128), BF),
            shape((K_ROWS, IDX), BF),
            shape((I_ROWS, IDX), BF),
        ),
        "pack",
        2 * 2 * n * 4 * 2048 * 64,
        jnp.swapaxes(q_latent, 1, 2).reshape(2 * WIDTH, HEADS),
        index_queries.reshape(2 * IH, IDX),
        index_weights,
        index_keys,
        key_scales.reshape(CHUNKS, 128),
        selected,
        wanted[0].T,
        specs=[HBM] * 7,
        limit=None,
        scratch=[
            pltpu.VMEM((2, IH), BF),
            pltpu.VMEM((CHUNKS, 128), BF),
            pltpu.VMEM(selected.shape, jnp.int32),
            pltpu.VMEM((wanted.shape[2], n), jnp.int32),
            pltpu.VMEM((2, n, LANES), F32),
            pltpu.SemaphoreType.DMA((8,)),
        ],
    )
    kv, q_wire = lax.optimization_barrier((kv, q_wire))
    q_far = permute(q_wire, lambda i: i ^ top)
    r2 = permute(kv, second)
    q_far, r2 = lax.optimization_barrier((q_far, r2))
    r3 = permute(r1, second)
    held = [(kv, (0, 0)), (r1, (2, 4)), (r2, (4, 2)), (r3, (6, 6))]
    for bit in range(3, bits - 1):
        step = 1 << bit
        held = held + [
            (permute(piece, lambda i: i ^ step), (a ^ step, b ^ step)) for piece, (a, b) in held
        ]

    k_next = permute(k_wire, lambda i: i ^ 2)
    kv_here, i_own, k_here = call(
        stage_kernel,
        (shape((WIDTH, TOK), BF), shape((I_ROWS, IDX), BF), shape((K_ROWS, IDX), BF)),
        "stage",
        0,
        kv,
        i_own,
        k_wire,
        specs=[HBM] * 3,
        scratch=[pltpu.SemaphoreType.DMA((3,))],
    )
    kv_core = swap(kv_here)
    keys = [k_here, swap(k_wire), k_next, swap(k_next)]

    def unpack(name, flops, *args):
        outs = [shape((ROWS, WIDTH), BF), shape((rows, TOK), F32)]
        if len(args) == 3:
            outs.append(shape((2 * I_ROWS, IDX), BF))
        return call(functools.partial(unpack_kernel, half_size), tuple(outs), name, flops, *args)

    q_far, *keys = lax.optimization_barrier((q_far, *keys))
    q_there, bias_there, i_pair = unpack("unpack_far", 3 * 1.15e9, q_far, q_far, i_own)
    q_here, bias_here = unpack("unpack_own", 0, q_wire, bias_own)

    def pair(item):
        piece, (a, b) = item
        return [item, (swap(piece), (1 ^ b, 1 ^ a))]

    def run(q, bias, groups, last, name, state=None):
        for k, group in enumerate(groups):
            mode = last if k == len(groups) - 1 else "state"
            state = attend(half_size, q, bias, group, state, mode, f"{name}_{k}")
        return state

    near = [[(kv_here, (0, 0)), (kv_core, (1, 1))]] + [pair(item) for item in held[1:3]]
    (own0, own1), (r1a, r1b), (r2a, r2b) = near
    far = attend(half_size, q_there, bias_there, [own0, own1, r1a, r2a], None, "state", "far_early")
    i_pairs = [i_pair]
    for bit in range(2, bits - 1):
        step = 1 << bit
        i_pairs = i_pairs + [permute(x, lambda i: i ^ step) for x in i_pairs]
    far, r3 = lax.optimization_barrier((far, r3))
    held[3] = (r3, held[3][1])
    late = [pair(item) for item in held[3:]]
    rest = sum(late[1:], [])
    groups = [[r1b, r2b, late[0][0]], [late[0][1]]]
    groups += [rest[at : at + 6] for at in range(0, len(rest), 6)]
    far = run(q_there, bias_there, groups[:-1], "state", "far_late", far)
    prepared = call(
        pairs_kernel,
        (shape((2 * I_W, IDX), BF), shape((2, IH, 16), F32)) * len(i_pairs),
        "index_pairs",
        6 * 1.15e9,
        *i_pairs,
    )
    *far, prepared = lax.optimization_barrier((*far, prepared))
    wire = attend(half_size, q_there, bias_there, groups[-1], far, "wire", "far_last")
    wire, lse_far = wire
    o_far = permute(wire, lambda i: i ^ top)

    parts = call(
        functools.partial(score_kernel, len(i_pairs)),
        tuple(shape((4, 4 * TOK), BF if j else F32) for j in range(len(i_pairs))),
        "index_scores",
        2 * len(i_pairs) * 4 * IH * 4 * TOK * IDX,
        *prepared,
        *keys,
    )
    parts = [[(part, 0)] for part in parts]
    for bit in reversed(range(2, bits - 1)):
        step = 1 << bit
        count = len(parts) // 2
        parts = [
            parts[j] + [(permute(x, lambda i: i ^ step), mask ^ step) for x, mask in parts[j + count]]
            for j in range(count)
        ]
    pieces = sum(near + late[:1], [])
    own = attend(half_size, q_here, bias_here, pieces[:4], None, "state", "own_first")
    ranges, own = lax.optimization_barrier((parts[0], own))
    o_own, lse_own = run(
        q_here, bias_here, [pieces[4:]] + groups[2:], "own", "own_late", own
    )
    scores_own, scores_far = call(
        functools.partial(order_kernel, half_size, tuple(mask for _, mask in parts[0])),
        (shape((2, half_size * TOK), F32), shape((2, half_size * TOK + 3 * HEADS), BF)),
        "order_scores",
        0,
        *[x for x, _ in ranges],
        lse_far,
    )
    scores_far = permute(scores_far, lambda i: i ^ top)

    return call(
        functools.partial(finish_kernel, half_size),
        (shape((2, n * TOK), F32), shape((2, HEADS, KVR), BF)),
        "finish",
        ROWS * KVR * 4,
        o_own,
        lse_own,
        o_far,
        scores_own,
        scores_far,
    )


def solution(mesh):
    spec = P(("groups", "ctx"))
    return jax.shard_map(
        functools.partial(local, mesh.shape["ctx"]),
        mesh=mesh,
        in_specs=(spec,) * 8,
        out_specs=(spec, spec),
        check_vma=False,
    )
```
